256 devices in a mesh: row: 16 (over y_hi, z), col: 16 (over x, y_lo, core).
Axes of the slice: x: 4, y: 4 (y_hi: 2, y_lo: 2; y = y_hi * 2 + y_lo), z: 8, core: 2. Of those that a mesh axis runs over, the one named last changes fastest.
Arguments:
- stack_embedding: bfloat16 [128, 640, 256], P('row', 'col'), may hold values from -6 to 6
- pair_representation: bfloat16 [640, 640, 128], P('row', 'col'), may hold values from -8 to 8
- mixing_entry_coefficients: bfloat16 [256, 1024], replicated, may hold values from -0.375 to 0.375
- mixing_final_coefficients: bfloat16 [256, 256], replicated, may hold values from -1 to 1
- pair_bias_matrix: bfloat16 [128, 8], replicated, may hold values from -4 to 4
- tensor_side_coefficients: bfloat16 [256, 64], replicated, may hold values from -0.375 to 0.375
- outer_output_weight: bfloat16 [1024, 128], replicated, may hold values from -1 to 1
- triangle_projection_weight: bfloat16 [128, 640], replicated, may hold values from -0.5 to 0.5
- triangle_output_weight: bfloat16 [128, 128], replicated, may hold values from -0.5 to 0.5
Outputs:
- stack_embedding_updated: bfloat16 [128, 640, 256], P('row', 'col')
- pair_state_next: bfloat16 [640, 640, 128], P('row', 'col')
The draws below stay inside these ranges and needn't reach their ends.
All inputs are finite; a program needn't handle non-finite values.
Results may differ from the reference program's by a relative error of at most 0.015.
Values may be sent and summed in bfloat16 or wider, within the bound.
A program may use at most 128 MiB of HBM per device.

```python
import jax
import jax.numpy as jnp
from jax import lax

STACK_FEATURES = 256
C_Z = 128
FOCUS_GROUPS = 8
PRODUCT_FACTORS = 32
FEATURE_WIDTH = 32
CHAIN_TOTAL = 128
POSITION_TOTAL = 640
ROWS_DEV = 40


def bias_table(draw_key):
    table_key = jax.random.fold_in(draw_key, 101)
    return jnp.clip(jax.random.normal(table_key, (C_Z, FOCUS_GROUPS), jnp.float32) * (2.0 * C_Z ** (-0.5)), -4.0, 4.0)


def draw_pair_bias_matrix(draw_key, part):
    return bias_table(draw_key).astype(jnp.bfloat16)


def draw_pair_representation(draw_key, part):
    noise_key = jax.random.fold_in(draw_key, 202)
    field = jax.random.normal(noise_key, (POSITION_TOTAL, POSITION_TOTAL, C_Z), jnp.float32)
    return jnp.clip(field, -8.0, 8.0).astype(jnp.bfloat16)


def block_scale(key, dims, split, smallest, high):
    factor_of, own = 1.0, jax.random.fold_in(key, 6)
    for dim, parts in split:
        steps = jnp.exp(jax.random.uniform(jax.random.fold_in(own, dim), (parts,), jnp.float32, smallest / len(split), high / len(split)))
        factor_of = factor_of * jnp.repeat(steps, dims[dim] // parts).reshape([-1 if axis == dim else 1 for axis in range(len(dims))])
    return factor_of


def gaussian(key, shape, deviation, bound, pieces=(), held_as=jnp.bfloat16):
    result = jax.random.normal(key, shape, jnp.float32) * deviation
    if len(pieces) > 0:
        result = block_scale(key, shape, pieces, -0.22, 0.18) * result
    return jnp.clip(result, min=-bound, max=bound).astype(held_as)


def setup_inputs(seed: int = 0) -> dict:
    key_list = jax.random.split(jax.random.key(seed), 10)
    stack_embedding = gaussian(key_list[0], (CHAIN_TOTAL, POSITION_TOTAL, STACK_FEATURES), 1.0, 6.0, ((0, 16), (1, 16)))
    pair_representation = draw_pair_representation(jax.random.fold_in(key_list[9], 71), 0)
    mixing_entry_coefficients = gaussian(key_list[2], (STACK_FEATURES, 4 * STACK_FEATURES), STACK_FEATURES ** -0.5, 0.375)
    mixing_final_coefficients = gaussian(key_list[3], (STACK_FEATURES, STACK_FEATURES), (STACK_FEATURES // 8) ** -0.5, 1.0)
    pair_bias_matrix = draw_pair_bias_matrix(jax.random.fold_in(key_list[9], 71), 0)
    tensor_side_coefficients = gaussian(key_list[5], (STACK_FEATURES, 2 * PRODUCT_FACTORS), STACK_FEATURES ** -0.5, 0.375)
    outer_output_weight = gaussian(key_list[6], (PRODUCT_FACTORS * PRODUCT_FACTORS, C_Z), PRODUCT_FACTORS ** -0.5, 1.0)
    triangle_projection_weight = gaussian(key_list[7], (C_Z, 5 * C_Z), C_Z ** -0.5, 0.5)
    triangle_output_weight = gaussian(key_list[8], (C_Z, C_Z), C_Z ** -0.5, 0.5)
    return dict(stack_embedding=stack_embedding, pair_representation=pair_representation, mixing_entry_coefficients=mixing_entry_coefficients, mixing_final_coefficients=mixing_final_coefficients, pair_bias_matrix=pair_bias_matrix, tensor_side_coefficients=tensor_side_coefficients, outer_output_weight=outer_output_weight, triangle_projection_weight=triangle_projection_weight, triangle_output_weight=triangle_output_weight)


epsilon = 1e-05

def standardize_features(inputs):
    inputs = inputs.astype(jnp.float32)
    center = inputs - lax.optimization_barrier(jnp.mean(inputs, axis=-1, keepdims=True))
    spread = lax.optimization_barrier(jnp.mean(center * center, axis=-1, keepdims=True))
    return center * lax.rsqrt(spread + epsilon)

def reference(stack_embedding, pair_representation, mixing_entry_coefficients, mixing_final_coefficients, pair_bias_matrix, tensor_side_coefficients, outer_output_weight, triangle_projection_weight, triangle_output_weight):
    stack_standardized = standardize_features(stack_embedding).astype(jnp.bfloat16).reshape(-1, STACK_FEATURES)
    mapped_lines = jnp.dot(stack_standardized, mixing_entry_coefficients, preferred_element_type=jnp.float32)
    stack_probe_vectors = (mapped_lines[:, :STACK_FEATURES] * FEATURE_WIDTH ** (-0.5)).astype(jnp.bfloat16).reshape(CHAIN_TOTAL, POSITION_TOTAL, FOCUS_GROUPS, FEATURE_WIDTH)
    stack_lookup_vectors = mapped_lines[:, STACK_FEATURES:2 * STACK_FEATURES].astype(jnp.bfloat16).reshape(CHAIN_TOTAL, POSITION_TOTAL, FOCUS_GROUPS, FEATURE_WIDTH)
    stack_content_vectors = mapped_lines[:, 2 * STACK_FEATURES:3 * STACK_FEATURES].astype(jnp.bfloat16).reshape(CHAIN_TOTAL, POSITION_TOTAL, FOCUS_GROUPS, FEATURE_WIDTH)
    sigmoid_factors = jax.nn.sigmoid(mapped_lines[:, 3 * STACK_FEATURES:]).reshape(CHAIN_TOTAL, POSITION_TOTAL, STACK_FEATURES)
    pair_normed = standardize_features(pair_representation).astype(jnp.bfloat16)
    pair_bias = jnp.einsum('ijc,ch->hij', pair_normed.astype(jnp.float32), pair_bias_matrix.astype(jnp.float32))
    pair_bias = lax.optimization_barrier(pair_bias.astype(jnp.bfloat16)).astype(jnp.float32)

    def lone_chain_lines(sequence_items):
        seq_query, seq_keys, seq_values = sequence_items
        scores = jnp.einsum('ihd,jhd->hij', seq_query.astype(jnp.float32), seq_keys.astype(jnp.float32)) + pair_bias
        row_peak = lax.optimization_barrier(jnp.max(scores, axis=-1, keepdims=True))
        exponent = jnp.exp(scores - row_peak)
        row_total = lax.optimization_barrier(jnp.sum(exponent, axis=-1))
        probs = lax.optimization_barrier(exponent.astype(jnp.bfloat16)).astype(jnp.float32)
        blended = jnp.einsum('hij,jhd->ihd', probs, seq_values.astype(jnp.float32))
        return blended / jnp.transpose(row_total)[..., None]
    weighted_mixture = lax.map(lone_chain_lines, (stack_probe_vectors, stack_lookup_vectors, stack_content_vectors)).reshape(CHAIN_TOTAL, POSITION_TOTAL, STACK_FEATURES)
    scaled_mixture = (sigmoid_factors * weighted_mixture).astype(jnp.bfloat16)
    stack_increment = jnp.dot(scaled_mixture.reshape(-1, STACK_FEATURES), mixing_final_coefficients, preferred_element_type=jnp.float32).reshape(CHAIN_TOTAL, POSITION_TOTAL, STACK_FEATURES)
    stack_embedding_updated = (stack_embedding.astype(jnp.float32) + stack_increment).astype(jnp.bfloat16)
    tensor_standardized = standardize_features(stack_embedding_updated).astype(jnp.bfloat16).reshape(-1, STACK_FEATURES)
    sides = jnp.dot(tensor_standardized, tensor_side_coefficients, preferred_element_type=jnp.float32).astype(jnp.bfloat16)
    sides = sides.reshape(CHAIN_TOTAL, POSITION_TOTAL, 2 * PRODUCT_FACTORS)
    left_side = sides[..., :PRODUCT_FACTORS]
    right_side = sides[..., PRODUCT_FACTORS:]
    left_blocks = jnp.transpose(left_side.reshape(CHAIN_TOTAL, POSITION_TOTAL // ROWS_DEV, ROWS_DEV, PRODUCT_FACTORS), (1, 0, 2, 3))

    def outer_block(left_block):
        products = jnp.einsum('sic,sjd->ijcd', left_block.astype(jnp.float32), right_side.astype(jnp.float32))
        averaged = (products * (1.0 / CHAIN_TOTAL)).astype(jnp.bfloat16)
        return jnp.dot(averaged.reshape(-1, PRODUCT_FACTORS * PRODUCT_FACTORS), outer_output_weight, preferred_element_type=jnp.float32).reshape(ROWS_DEV, POSITION_TOTAL, C_Z)
    outer_update = lax.map(outer_block, left_blocks).reshape(POSITION_TOTAL, POSITION_TOTAL, C_Z)
    pair_mid = (pair_representation.astype(jnp.float32) + outer_update).astype(jnp.bfloat16)
    tri_normed = standardize_features(pair_mid).astype(jnp.bfloat16).reshape(-1, C_Z)

    def project(block_index):
        columns = triangle_projection_weight[:, block_index * C_Z:(block_index + 1) * C_Z]
        return jnp.dot(tri_normed, columns, preferred_element_type=jnp.float32).reshape(POSITION_TOTAL, POSITION_TOTAL, C_Z)
    left_edge = (jax.nn.sigmoid(project(1)) * project(0)).astype(jnp.bfloat16)
    right_edge = (jax.nn.sigmoid(project(3)) * project(2)).astype(jnp.bfloat16)
    out_gate = jax.nn.sigmoid(project(4))
    summed = jnp.einsum('ikc,jkc->ijc', left_edge.astype(jnp.float32), right_edge.astype(jnp.float32))
    tri_ln = standardize_features(summed).astype(jnp.bfloat16)
    tri_update = jnp.dot(tri_ln.reshape(-1, C_Z), triangle_output_weight, preferred_element_type=jnp.float32).reshape(POSITION_TOTAL, POSITION_TOTAL, C_Z)
    pair_state_next = (pair_mid.astype(jnp.float32) + out_gate * tri_update).astype(jnp.bfloat16)
    return (stack_embedding_updated, pair_state_next)
```

```python
import functools

import jax
import jax.numpy as jnp
from jax import lax
from jax.experimental import pallas as pl
from jax.experimental.pallas import tpu as pltpu
from jax.sharding import PartitionSpec as P

MESH = pl.DeviceIdType.MESH
EPS = 1e-05
N = 16
BF = jnp.bfloat16
F32 = jnp.float32


def standardize(v, axis=-1):
    v = v.astype(F32)
    center = v - jnp.mean(v, axis=axis, keepdims=True)
    spread = jnp.mean(center * center, axis=axis, keepdims=True)
    return center * lax.rsqrt(spread + EPS)


def here():
    return lax.axis_index("row"), lax.axis_index("col")


def push(src, dst, send, recv, to):
    pltpu.make_async_remote_copy(src, dst, send, recv, device_id=to, device_id_type=MESH).start()


def local(src, dst, recv):
    pltpu.make_async_copy(src, dst, recv).start()


def drain(ref, sem):
    pltpu.make_async_copy(ref, ref, sem).wait()


def greet(to):
    pl.semaphore_signal(pltpu.get_barrier_semaphore(), inc=1, device_id=to, device_id_type=MESH)


def greeted(count):
    pl.semaphore_wait(pltpu.get_barrier_semaphore(), count)


def turned_greet(by_row):
    r, c = here()
    for s in range(N):
        k = lax.rem(c + s, N)
        to = (c, k) if by_row else (k, r)

        @pl.when((c != r) | (k != c))
        def _():
            greet(to)


def turned_push(src, dst, send, recv, by_row):
    r, c = here()
    slot = dst.at[c] if by_row else dst.at[r]
    for s in range(N):
        k = lax.rem(r + s, N)
        own = (k == r) & (r == c)
        to = (k, r) if by_row else (c, k)

        @pl.when(jnp.logical_not(own))
        def _():
            push(src, slot, send, recv, to)

        @pl.when(own)
        def _():
            local(src, slot, recv)


def turned_sent(dst, send):
    r, c = here()
    drain(dst.at[pl.ds(0, N - 1)], send)

    @pl.when(r != c)
    def _():
        drain(dst.at[0], send)


def comm_call(body, name, collective_id, outs, ins, sems, scratch=()):
    return pl.pallas_call(
        body,
        name=name,
        out_shape=outs,
        in_specs=[pl.BlockSpec(memory_space=pltpu.VMEM)] * len(ins),
        out_specs=jax.tree.map(lambda _: pl.BlockSpec(memory_space=pltpu.VMEM), outs),
        scratch_shapes=[pltpu.SemaphoreType.DMA((sems,)), *scratch],
        compiler_params=pltpu.CompilerParams(
            collective_id=collective_id, has_side_effects=True, vmem_limit_bytes=48 << 20
        ),
    )(*ins)


def entry_body(x, bias, xs, biases, sem):
    r, c = here()
    core = lax.rem(c, 2)
    mate = c + 1 - 2 * core
    for s in range(1, 8):
        greet((r, lax.rem(c + 2 * s, N)))
    greet((r, mate))
    turned_greet(True)
    greeted(8 + 15 + jnp.where(r == c, 0, 1))

    for s in range(1, 8):
        push(x, xs.at[c], sem.at[0], sem.at[2 + s], (r, lax.rem(c + 2 * s, N)))
    push(x, xs.at[c], sem.at[10], sem.at[2], (r, mate))
    local(x, xs.at[c], sem.at[11])
    turned_push(bias, biases, sem.at[12], sem.at[13], True)
    for s in range(1, 8):
        source = lax.rem(c - 2 * s + 2 * N, N)
        drain(xs.at[source], sem.at[2 + s])
        push(xs.at[source], xs.at[source], sem.at[10], sem.at[2], (r, mate))
    drain(xs.at[pl.ds(0, 7)], sem.at[0])
    drain(xs.at[pl.ds(0, 8)], sem.at[10])
    drain(xs.at[pl.ds(0, 8)], sem.at[2])
    drain(xs.at[0], sem.at[11])
    turned_sent(biases, sem.at[12])
    drain(biases, sem.at[13])


def sides_body(left, right, lefts, rights, sem):
    r, c = here()
    for s in range(1, N):
        greet((lax.rem(r + s, N), c))
    turned_greet(False)
    greeted(15 + 15 + jnp.where(r == c, 0, 1))

    turned_push(left, lefts, sem.at[0], sem.at[1], False)
    for s in range(1, N):
        push(right, rights.at[r], sem.at[2], sem.at[3], (lax.rem(r + s, N), c))
    local(right, rights.at[r], sem.at[3])
    turned_sent(lefts, sem.at[0])
    drain(lefts, sem.at[1])
    drain(rights.at[pl.ds(0, N - 1)], sem.at[2])
    drain(rights, sem.at[3])


def over_col_body(left, right, got, sem):
    r, c = here()
    side = lax.rem(r, 2)
    for s in range(1, N):
        greet((r, lax.rem(c + s, N)))
    greeted(15)
    for s in range(8):
        g = lax.rem(c // 2 + s, 8)
        for ref, to in ((left, 2 * g + 1 - side), (right, 2 * g + side)):
            if s == 0:

                @pl.when(to != c)
                def _():
                    push(ref.at[g], got.at[c], sem.at[0], sem.at[1], (r, to))

                @pl.when(to == c)
                def _():
                    local(ref.at[g], got.at[c], sem.at[1])
            else:
                push(ref.at[g], got.at[c], sem.at[0], sem.at[1], (r, to))
    drain(got.at[pl.ds(0, N - 1)], sem.at[0])
    drain(got, sem.at[1])


def over_row_body(parts, got, mates, sem):
    r, c = here()
    core = lax.rem(c, 2)
    mate = c + 1 - 2 * core
    kind = lax.rem(r + core, 2)
    for s in range(1, N):
        greet((lax.rem(r + s, N), c))
    greet((r, mate))
    greeted(16)
    for s in range(1, N):
        q = lax.rem(r + s, N)
        push(parts.at[q], got.at[kind, r // 2], sem.at[0], sem.at[1 + lax.rem(r, 2)], (q, c))
    local(parts.at[r], got.at[kind, r // 2], sem.at[1 + lax.rem(r, 2)])
    drain(got.at[1], sem.at[2 - core])
    push(got.at[1], mates, sem.at[3], sem.at[4], (r, mate))
    drain(parts.at[pl.ds(0, N - 1)], sem.at[0])
    drain(got.at[0], sem.at[1 + core])
    drain(mates, sem.at[3])
    drain(mates, sem.at[4])


def back_row_body(parts, got, sem):
    r, c = here()
    for s in range(1, N):
        greet((lax.rem(r + s, N), c))
    greeted(15)
    for s in range(1, N):
        q = lax.rem(r + s, N)
        push(parts.at[q], got.at[r], sem.at[0], sem.at[1], (q, c))
    local(parts.at[r], got.at[r], sem.at[1])
    drain(parts.at[pl.ds(0, N - 1)], sem.at[0])
    drain(got, sem.at[1])


def back_col_body(parts, got, sem):
    r, c = here()
    core = lax.rem(c, 2)
    mine = c // 2
    for s in range(1, 8):
        greet((r, lax.rem(c + 2 * s, N)))
    greeted(7)
    for s in range(1, 8):
        g = lax.rem(mine + s, 8)
        push(parts.at[g], got.at[mine], sem.at[0], sem.at[1], (r, 2 * g + core))
    local(parts.at[mine], got.at[mine], sem.at[1])
    drain(parts.at[pl.ds(0, 7)], sem.at[0])
    drain(got, sem.at[1])


def like(shape, dtype=BF):
    return jax.ShapeDtypeStruct(shape, dtype)


def shards(x, pair, w_in, w_out, w_bias, w_sides, w_outer, w_tri, w_tri_out):
    core = lax.rem(lax.axis_index("col"), 2)
    S, B, C = x.shape
    Z = pair.shape[2]
    H = w_bias.shape[1]
    D = C // H
    O = w_sides.shape[1] // 2
    SP = S * N
    R = B * N

    pair_n = standardize(pair).astype(BF).reshape(B * B, Z)
    bias = jnp.einsum("ch,pc->hp", w_bias, pair_n, preferred_element_type=F32).astype(BF)
    xs, biases = comm_call(
        entry_body, "entry_exchange", 1, [like((N, S, B, C)), like((N, H, B * B))], [x, bias], 14
    )
    biases = biases.reshape(N, H, B, B).transpose(1, 2, 0, 3).reshape(H, B, R)
    own_n = standardize(x).astype(BF).reshape(-1, C)
    all_n = standardize(xs).astype(BF).transpose(1, 0, 2, 3).reshape(-1, C)
    own = jnp.dot(own_n, jnp.concatenate([w_in[:, :C], w_in[:, 3 * C :]], 1), preferred_element_type=F32)
    kv = jnp.dot(all_n, w_in[:, C : 3 * C], preferred_element_type=F32).astype(BF)
    q = (own[:, :C] * D ** (-0.5)).astype(BF).reshape(S, B, H, D)
    gate = jax.nn.sigmoid(own[:, C:]).reshape(S, B, C)
    k = kv[:, :C].reshape(S, R, H, D)
    v = kv[:, C:].reshape(S, R, H, D)
    scores = jnp.einsum("sihd,sjhd->shij", q, k, preferred_element_type=F32) + biases.astype(F32)
    peak = jnp.max(scores, -1, keepdims=True)
    e = jnp.exp(scores - peak)
    total = jnp.sum(e, -1)
    att = jnp.einsum("shij,sjhd->sihd", e.astype(BF), v, preferred_element_type=F32)
    att = (att / jnp.transpose(total, (0, 2, 1))[..., None]).reshape(S, B, C)
    gated = (gate * att).astype(BF)
    x_new = (
        x.astype(F32)
        + jnp.dot(gated.reshape(-1, C), w_out, preferred_element_type=F32).reshape(S, B, C)
    ).astype(BF)
    sides = jnp.dot(
        standardize(x_new).astype(BF).reshape(-1, C), w_sides, preferred_element_type=F32
    ).astype(BF).reshape(S, B, 2 * O)
    left, right = sides[..., :O].reshape(S, B * O), sides[..., O:].reshape(S, B * O)
    lefts, rights = comm_call(
        sides_body, "sides_exchange", 2, [like((N, S, B * O))] * 2, [left, right], 4
    )
    lefts = lefts.reshape(SP, B, O)
    rights = rights.reshape(SP, B, O)
    products = jnp.einsum("sic,sjd->ijcd", lefts, rights, preferred_element_type=F32)
    averaged = (products * (1.0 / SP)).astype(BF).reshape(B * B, O * O)
    pair_mid = (
        pair.astype(F32) + jnp.dot(averaged, w_outer, preferred_element_type=F32).reshape(B, B, Z)
    ).astype(BF)
    tri_n = standardize(pair_mid).astype(BF).reshape(B * B, Z)
    edges = jnp.einsum("cn,pc->np", w_tri[:, : 4 * Z], tri_n, preferred_element_type=F32)
    left_edge = (jax.nn.sigmoid(edges[Z : 2 * Z]) * edges[:Z]).astype(BF)
    right_edge = (jax.nn.sigmoid(edges[3 * Z :]) * edges[2 * Z : 3 * Z]).astype(BF)
    out_gate = jax.nn.sigmoid(jnp.dot(tri_n, w_tri[:, 4 * Z :], preferred_element_type=F32))
    got = comm_call(
        over_col_body, "edges_over_col", 3, like((N, N, B * B)),
        [left_edge.reshape(8, N, B * B), right_edge.reshape(8, N, B * B)], 2,
    )
    parts = got.reshape(N, N, B, B).transpose(1, 2, 0, 3).reshape(N, B, R)
    got, mates = comm_call(
        over_row_body, "edges_over_row", 4, [like((2, 8, B, R)), like((8, B, R))], [parts], 5
    )
    r_all = got[0].reshape(8 * B, R)
    l_other = jnp.dot(got[1].reshape(8 * B, R), r_all.T, preferred_element_type=F32).astype(BF)
    l_same = jnp.dot(mates.reshape(8 * B, R), r_all.T, preferred_element_type=F32).astype(BF)
    l_other, l_same = l_other.reshape(8, B, 8 * B), l_same.reshape(8, B, 8 * B)
    even = jnp.where(core == 0, l_same, l_other)
    odd = jnp.where(core == 0, l_other, l_same)
    sums = jnp.stack([even, odd], 1).reshape(N, B, 8 * B)
    got = comm_call(back_row_body, "sums_over_row", 5, like(sums.shape), [sums], 2)
    parts = got.reshape(N, B, 8, B).transpose(2, 0, 1, 3).reshape(8, N, B * B)
    got = comm_call(back_col_body, "sums_over_col", 6, like(parts.shape), [parts], 2)
    tri_ln = standardize(got.reshape(Z, B * B), 0).astype(BF)
    update = jnp.einsum("cp,cn->pn", tri_ln, w_tri_out, preferred_element_type=F32)
    pair_new = (pair_mid.astype(F32) + (out_gate * update).reshape(B, B, Z)).astype(BF)
    return x_new, pair_new


def solution(mesh):
    tile = P("row", "col", None)
    return jax.shard_map(
        shards,
        mesh=mesh,
        in_specs=(tile, tile) + (P(),) * 7,
        out_specs=(tile, tile),
        check_vma=False,
    )
```

```python
import functools

import jax
import jax.numpy as jnp
from jax import lax
from jax.experimental import pallas as pl
from jax.experimental.pallas import tpu as pltpu
from jax.sharding import PartitionSpec as P

MESH = pl.DeviceIdType.MESH
EPS = 1e-05
N = 16
BF = jnp.bfloat16
F32 = jnp.float32


def standardize(v, axis=-1):
    v = v.astype(F32)
    center = v - jnp.mean(v, axis=axis, keepdims=True)
    spread = jnp.mean(center * center, axis=axis, keepdims=True)
    return center * lax.rsqrt(spread + EPS)


def here():
    return lax.axis_index("row"), lax.axis_index("col")


def push(src, dst, send, recv, to):
    pltpu.make_async_remote_copy(src, dst, send, recv, device_id=to, device_id_type=MESH).start()


def local(src, dst, recv):
    pltpu.make_async_copy(src, dst, recv).start()


def drain(ref, sem):
    pltpu.make_async_copy(ref, ref, sem).wait()


def greet(to):
    pl.semaphore_signal(pltpu.get_barrier_semaphore(), inc=1, device_id=to, device_id_type=MESH)


def greeted(count):
    pl.semaphore_wait(pltpu.get_barrier_semaphore(), count)


def turned_greet(by_row):
    r, c = here()
    for s in range(N):
        k = lax.rem(c + s, N)
        to = (c, k) if by_row else (k, r)

        @pl.when((c != r) | (k != c))
        def _():
            greet(to)


def turned_push(src, dst, send, recv, by_row):
    r, c = here()
    slot = dst.at[c] if by_row else dst.at[r]
    for s in range(N):
        k = lax.rem(r + s, N)
        own = (k == r) & (r == c)
        to = (k, r) if by_row else (c, k)

        @pl.when(jnp.logical_not(own))
        def _():
            push(src, slot, send, recv, to)

        @pl.when(own)
        def _():
            local(src, slot, recv)


def turned_sent(dst, send):
    r, c = here()
    drain(dst.at[pl.ds(0, N - 1)], send)

    @pl.when(r != c)
    def _():
        drain(dst.at[0], send)


def comm_call(body, name, collective_id, outs, ins, sems, scratch=()):
    return pl.pallas_call(
        body,
        name=name,
        out_shape=outs,
        in_specs=[pl.BlockSpec(memory_space=pltpu.VMEM)] * len(ins),
        out_specs=jax.tree.map(lambda _: pl.BlockSpec(memory_space=pltpu.VMEM), outs),
        scratch_shapes=[*scratch, pltpu.SemaphoreType.DMA((sems,))],
        compiler_params=pltpu.CompilerParams(
            collective_id=collective_id, has_side_effects=True, vmem_limit_bytes=48 << 20
        ),
    )(*ins)


def attention_body(
    x, pair, w_in, w_out, w_bias, x_new, xs, bias_out, biases, bias, q_all, gates, sem
):
    r, c = here()
    core = lax.rem(c, 2)
    mate = c + 1 - 2 * core
    S, B, C = x.shape
    H = w_bias.shape[1]
    D = C // H
    for s in range(1, 8):
        greet((r, lax.rem(c + 2 * s, N)))
    greet((r, mate))
    turned_greet(True)
    greeted(8 + 15 + jnp.where(r == c, 0, 1))
    for s in range(1, 8):
        push(x, xs.at[c], sem.at[0], sem.at[2 + s], (r, lax.rem(c + 2 * s, N)))
    push(x, xs.at[c], sem.at[10], sem.at[2], (r, mate))
    local(x, xs.at[c], sem.at[11])
    pair_n = standardize(pair[...]).astype(BF).reshape(B * B, pair.shape[2])
    bias_out[...] = lax.dot_general(
        w_bias[...], pair_n, (((0,), (1,)), ((), ())), preferred_element_type=F32
    ).astype(BF)
    turned_push(bias_out, biases, sem.at[12], sem.at[13], True)
    own_n = standardize(x[...]).astype(BF).reshape(S * B, C)
    q = jnp.dot(own_n, w_in[:, :C], preferred_element_type=F32) * D ** (-0.5)
    q_all[...] = q.reshape(S, B, C)
    gates[...] = jax.nn.sigmoid(
        jnp.dot(own_n, w_in[:, 3 * C :], preferred_element_type=F32)
    ).reshape(S, B, C)
    for s in range(1, 8):
        source = lax.rem(c - 2 * s + 2 * N, N)
        drain(xs.at[source], sem.at[2 + s])
        push(xs.at[source], xs.at[source], sem.at[10], sem.at[2], (r, mate))
    turned_sent(biases, sem.at[12])
    drain(biases, sem.at[13])
    spread(lambda k: biases[k].astype(F32), bias, B)
    drain(xs.at[pl.ds(0, 7)], sem.at[0])
    drain(xs.at[pl.ds(0, 8)], sem.at[10])
    drain(xs.at[pl.ds(0, 8)], sem.at[2])
    drain(xs.at[0], sem.at[11])
    head = lax.broadcasted_iota(jnp.int32, (B, C), 1) // D

    @pl.loop(0, S)
    def _(s):
        x_s = standardize(xs[:, s]).reshape(N * B, C).astype(BF)
        k = jnp.dot(x_s, w_in[:, C : 2 * C], preferred_element_type=F32).astype(BF)
        v = jnp.dot(x_s, w_in[:, 2 * C : 3 * C], preferred_element_type=F32).astype(BF)
        q_s = q_all[s]
        q_h = jnp.concatenate([jnp.where(head == h, q_s, 0.0) for h in range(H)], 0).astype(BF)
        scores = lax.dot_general(
            q_h, k, (((1,), (1,)), ((), ())), preferred_element_type=F32
        ) + bias[...].reshape(H * B, N * B)
        e = jnp.exp(scores - jnp.max(scores, -1, keepdims=True))
        att = jnp.dot(e.astype(BF), v, preferred_element_type=F32)
        att = (att / jnp.sum(e, -1, keepdims=True)).reshape(H, B, C)
        total = jnp.where(head == 0, att[0], 0.0)
        for h in range(1, H):
            total = jnp.where(head == h, att[h], total)
        gated = (gates[s] * total).astype(BF)
        x_new[s] = (
            x[s].astype(F32) + jnp.dot(gated, w_out[...], preferred_element_type=F32)
        ).astype(BF)


def spread(block, out, B):
    blocks = [block(k) for k in range(N)]
    for i in range(B):
        out[:, i, :] = jnp.concatenate([b[:, i * B : (i + 1) * B] for b in blocks], 1)


def outer_body(
    x_new, pair, w_sides, w_outer, w_tri, got, mid, gate,
    by_residue, left, right, lefts, rights, tall, stacked, w_wide, normed, left_edge, right_edge, sem,
):
    r, c = here()
    S, B, C = x_new.shape
    O = w_sides.shape[1] // 2
    Z = pair.shape[2]
    for s in range(1, N):
        greet((lax.rem(r + s, N), c))
    turned_greet(False)
    for s in range(1, N):
        greet((r, lax.rem(c + s, N)))
    sides = jnp.dot(
        standardize(x_new[...]).astype(BF).reshape(S * B, C), w_sides[...], preferred_element_type=F32
    )
    for s in range(S):
        by_residue[:, s, : 2 * O] = sides[s * B : (s + 1) * B]
    left[...] = jnp.concatenate([by_residue[i, :, :O] for i in range(B)], 1).astype(BF)
    right[...] = jnp.concatenate([by_residue[i, :, O : 2 * O] for i in range(B)], 1).astype(BF)
    greeted(45 + jnp.where(r == c, 0, 1))
    turned_push(left, lefts, sem.at[0], sem.at[1], False)
    for s in range(1, N):
        push(right, rights.at[r], sem.at[2], sem.at[3], (lax.rem(r + s, N), c))
    local(right, rights.at[r], sem.at[3])

    w_wide[...] = jnp.zeros_like(w_wide)
    tall[pl.ds(0, O * O), :] = w_outer[...].astype(F32)
    for d in range(O):
        part = tall[pl.ds(d, O, stride=O), :].astype(BF)
        for i in range(4):
            w_wide[pl.ds(d * 4 * O + i * O, O), i * Z : (i + 1) * Z] = part
    turned_sent(lefts, sem.at[0])
    drain(lefts, sem.at[1])
    drain(rights.at[pl.ds(0, N - 1)], sem.at[2])
    drain(rights, sem.at[3])

    tall[...] = rights[...].reshape(S * N, B * O).astype(F32).T
    right_t = jnp.concatenate([tall[pl.ds(d, B, stride=O), :] for d in range(O)], 0).astype(BF)
    left_s = lefts[...].reshape(S * N, B * O)
    for g in range(B // 8):
        halves = [
            jnp.dot(
                right_t, left_s[:, k * 4 * O : (k + 1) * 4 * O], preferred_element_type=F32
            ) * (1.0 / (S * N))
            for k in (2 * g, 2 * g + 1)
        ]
        for d in range(O):
            stacked[pl.ds(g * 2 * B, 2 * B), d * 4 * O : (d + 1) * 4 * O] = jnp.concatenate(
                [h[d * B : (d + 1) * B] for h in halves], 0
            ).astype(BF)
    wide = jnp.dot(stacked[...], w_wide[...], preferred_element_type=F32)
    for i in range(B):
        k, u = i // 4, i % 4
        row = (pair[i].astype(F32) + wide[k * B : (k + 1) * B, u * Z : (u + 1) * Z]).astype(BF)
        mid[i] = row
        normed[pl.ds(i * B, B), :] = standardize(row)
    tri_n = normed[...].astype(BF)

    def edge(k):
        w = w_tri[:, 2 * k * Z : 2 * (k + 1) * Z]
        both = lax.dot_general(w, tri_n, (((0,), (1,)), ((), ())), preferred_element_type=F32)
        return (jax.nn.sigmoid(both[Z:]) * both[:Z]).astype(BF).reshape(8, N, B * B)

    parity = lax.rem(r, 2)
    for k, ref in ((0, left_edge), (1, right_edge)):
        ref[...] = edge(k)
        for s in range(8):
            g = lax.rem(c // 2 + s, 8)
            to = 2 * g + lax.rem(parity + 1 + k, 2)
            if s == 0:

                @pl.when(to != c)
                def _():
                    push(ref.at[g], got.at[c], sem.at[4], sem.at[5], (r, to))

                @pl.when(to == c)
                def _():
                    local(ref.at[g], got.at[c], sem.at[5])
            else:
                push(ref.at[g], got.at[c], sem.at[4], sem.at[5], (r, to))
    gate[...] = jax.nn.sigmoid(jnp.dot(tri_n, w_tri[:, 4 * Z :], preferred_element_type=F32))
    drain(got.at[pl.ds(0, N - 1)], sem.at[4])
    drain(got, sem.at[5])


def triangle_body(
    edges, mid, gate, w, out, spreads, parts, got, mates, sums, channel, back, flat, tiles, sem
):
    r, c = here()
    core = lax.rem(c, 2)
    mate = c + 1 - 2 * core
    mine = c // 2
    B = mid.shape[0]
    Z = mid.shape[2]
    R = N * B
    kind = lax.rem(r + core, 2)
    for s in range(1, N):
        greet((lax.rem(r + s, N), c))
    greet((r, mate))
    for s in range(1, 8):
        greet((r, lax.rem(c + 2 * s, N)))
    for h in range(2):
        spread(lambda k: edges[k].astype(F32)[8 * h : 8 * h + 8], spreads, B)
        parts[pl.ds(8 * h, 8)] = spreads[...].astype(BF)
        if h == 0:
            greeted(23)
        arrived = sem.at[1 + lax.rem(r, 2)]
        for s in range(8):
            q = 8 * h + lax.rem(r + s, 8)
            if s == 0:

                @pl.when(q != r)
                def _():
                    push(parts.at[q], got.at[kind, r // 2], sem.at[0], arrived, (q, c))

                @pl.when(q == r)
                def _():
                    local(parts.at[q], got.at[kind, r // 2], arrived)
            else:
                push(parts.at[q], got.at[kind, r // 2], sem.at[0], arrived, (q, c))
    drain(got.at[1], sem.at[2 - core])
    push(got.at[1], mates, sem.at[3], sem.at[4], (r, mate))
    drain(got.at[0], sem.at[1 + core])
    columns = got[0].reshape(8 * B, R)
    for rows, parity in ((got.at[1], 1 - core), (mates, core)):
        if rows is mates:
            drain(mates, sem.at[4])
        total = lax.dot_general(
            rows[...].reshape(8 * B, R), columns, (((1,), (1,)), ((), ())), preferred_element_type=F32
        )
        for s in range(8):
            q = 2 * s + parity
            sums[q] = total[s * B : (s + 1) * B].astype(BF)

            @pl.when(q != r)
            def _():
                push(sums.at[q], channel.at[r], sem.at[5], sem.at[6], (q, c))

            @pl.when(q == r)
            def _():
                local(sums.at[q], channel.at[r], sem.at[6])
    drain(parts.at[pl.ds(0, N - 1)], sem.at[0])
    drain(mates, sem.at[3])
    drain(sums.at[pl.ds(0, N - 1)], sem.at[5])
    drain(channel, sem.at[6])
    back[...] = channel[...].astype(F32)
    rows = [back[:, i, :] for i in range(B)]
    for g in range(8):
        flat[g] = jnp.concatenate([v[:, g * B : (g + 1) * B] for v in rows], 1).astype(BF)
    for s in range(1, 8):
        g = lax.rem(mine + s, 8)
        push(flat.at[g], tiles.at[mine], sem.at[7], sem.at[8], (r, 2 * g + core))
    local(flat.at[mine], tiles.at[mine], sem.at[8])
    drain(flat.at[pl.ds(0, 7)], sem.at[7])
    drain(tiles, sem.at[8])
    tri_ln = standardize(tiles[...].reshape(Z, B * B), 0).astype(BF)
    update = lax.dot_general(
        tri_ln, w[...], (((0,), (0,)), ((), ())), preferred_element_type=F32
    )
    out[...] = (mid[...].astype(F32) + (gate[...] * update).reshape(B, B, Z)).astype(BF)


def like(shape, dtype=BF):
    return jax.ShapeDtypeStruct(shape, dtype)


def shards(x, pair, w_in, w_out, w_bias, w_sides, w_outer, w_tri, w_tri_out):
    core = lax.rem(lax.axis_index("col"), 2)
    S, B, C = x.shape
    Z = pair.shape[2]
    H = w_bias.shape[1]
    D = C // H
    O = w_sides.shape[1] // 2
    SP = S * N
    R = B * N

    VM = pltpu.VMEM
    x_new = comm_call(
        attention_body, "attention", 1, like((S, B, C)), [x, pair, w_in, w_out, w_bias], 14,
        [VM((N, S, B, C), BF), VM((H, B * B), BF), VM((N, H, B * B), BF), VM((H, B, R), F32),
         VM((S, B, C), F32), VM((S, B, C), F32)],
    )
    edges, mid, gate = comm_call(
        outer_body, "outer", 2,
        [like((N, N, B * B)), like((B, B, Z)), like((B * B, Z), F32)],
        [x_new, pair, w_sides, w_outer, w_tri], 6,
        [VM((B, S, 128), F32), VM((S, B * O), BF), VM((S, B * O), BF), VM((N, S, B * O), BF),
         VM((N, S, B * O), BF), VM((B * O, SP), F32), VM((10 * B, 4 * O * O), BF),
         VM((4 * O * O, 4 * Z), BF), VM((B * B, Z), F32), VM((8, N, B * B), BF), VM((8, N, B * B), BF)],
    )
    pair_new = comm_call(
        triangle_body, "triangle", 3, like((B, B, Z)), [edges, mid, gate, w_tri_out], 9,
        [VM((8, B, R), F32), VM((N, B, R), BF), VM((2, 8, B, R), BF), VM((8, B, R), BF),
         VM((N, B, 8 * B), BF), VM((N, B, 8 * B), BF), VM((N, B, 8 * B), F32), VM((8, N, B * B), BF),
         VM((8, N, B * B), BF)],
    )
    return x_new, pair_new


def solution(mesh):
    tile = P("row", "col", None)
    return jax.shard_map(
        shards,
        mesh=mesh,
        in_specs=(tile, tile) + (P(),) * 7,
        out_specs=(tile, tile),
        check_vma=False,
    )
```

```python
import functools

import jax
import jax.numpy as jnp
from jax import lax
from jax.experimental import pallas as pl
from jax.experimental.pallas import tpu as pltpu
from jax.sharding import PartitionSpec as P

MESH = pl.DeviceIdType.MESH
EPS = 1e-05
N = 16
BF = jnp.bfloat16
F32 = jnp.float32


def standardize(v, axis=-1):
    v = v.astype(F32)
    center = v - jnp.mean(v, axis=axis, keepdims=True)
    spread = jnp.mean(center * center, axis=axis, keepdims=True)
    return center * lax.rsqrt(spread + EPS)


def here():
    return lax.axis_index("row"), lax.axis_index("col")


def push(src, dst, send, recv, to):
    pltpu.make_async_remote_copy(src, dst, send, recv, device_id=to, device_id_type=MESH).start()


def local(src, dst, recv):
    pltpu.make_async_copy(src, dst, recv).start()


def drain(ref, sem):
    pltpu.make_async_copy(ref, ref, sem).wait()


def greet(to):
    pl.semaphore_signal(pltpu.get_barrier_semaphore(), inc=1, device_id=to, device_id_type=MESH)


def greeted(count):
    pl.semaphore_wait(pltpu.get_barrier_semaphore(), count)


def turned_greet():
    r, c = here()
    for s in range(N):
        k = lax.rem(c + s, N)

        @pl.when((c != r) | (k != c))
        def _():
            greet((c, k))


def turned_push(src, dst, send, recv):
    r, c = here()
    for s in range(N):
        k = lax.rem(r + c + s, N)
        own = (k == r) & (r == c)

        @pl.when(jnp.logical_not(own))
        def _():
            push(src, dst.at[c], send, recv, (k, r))

        @pl.when(own)
        def _():
            local(src, dst.at[c], recv)


def turned_sent(dst, send):
    r, c = here()
    drain(dst.at[pl.ds(0, N - 1)], send)

    @pl.when(r != c)
    def _():
        drain(dst.at[0], send)


def comm_call(body, name, collective_id, outs, ins, sems, scratch=()):
    return pl.pallas_call(
        body,
        name=name,
        out_shape=outs,
        in_specs=[pl.BlockSpec(memory_space=pltpu.VMEM)] * len(ins),
        out_specs=jax.tree.map(lambda _: pl.BlockSpec(memory_space=pltpu.VMEM), outs),
        scratch_shapes=[*scratch, pltpu.SemaphoreType.DMA((sems,))],
        compiler_params=pltpu.CompilerParams(
            collective_id=collective_id, has_side_effects=True, vmem_limit_bytes=48 << 20
        ),
    )(*ins)


def attention_body(
    x, pair, w_in, w_out, w_bias, x_new, xs, bias_out, biases, bias, q_all, gates, near, far, sem
):
    r, c = here()
    core = lax.rem(c, 2)
    mate = c + 1 - 2 * core
    S, B, C = x.shape
    H = w_bias.shape[0]
    D = C // H
    mine = c // 2
    for s in range(1, 8):
        greet((r, lax.rem(c + 2 * s, N)))
    greet((r, mate))
    turned_greet()
    pair_n = standardize(pair[...]).astype(BF).reshape(B * B, pair.shape[2])
    bias_out[...] = lax.dot_general(
        w_bias[...], pair_n, (((1,), (1,)), ((), ())), preferred_element_type=F32
    ).astype(BF)
    greeted(8 + 15 + jnp.where(r == c, 0, 1))
    turned_push(bias_out, biases, sem.at[0], sem.at[1])

    @pl.loop(0, S)
    def _(s):
        for g in range(1, 8):
            push(x.at[s], xs.at[s, core, mine], sem.at[2], near.at[s], (r, lax.rem(c + 2 * g, N)))
        local(x.at[s], xs.at[s, core, mine], near.at[s])

    def forward(s):
        drain(xs.at[s, core], near.at[s])
        push(xs.at[s, core], xs.at[s, core], sem.at[3], far.at[s], (r, mate))

    own_n = standardize(x[...]).astype(BF).reshape(S * B, C)
    q = jnp.dot(own_n, w_in[:, :C], preferred_element_type=F32) * D ** (-0.5)
    q_all[...] = q.reshape(S, B, C)
    gates[...] = jax.nn.sigmoid(
        jnp.dot(own_n, w_in[:, 3 * C :], preferred_element_type=F32)
    ).reshape(S, B, C)
    forward(0)
    turned_sent(biases, sem.at[0])
    drain(biases, sem.at[1])
    spread(lambda k: biases[2 * (k % 8) + k // 8].astype(F32), bias, B)
    head = lax.broadcasted_iota(jnp.int32, (B, C), 1) // D

    @pl.loop(0, S)
    def _(s):
        @pl.when(s < S - 1)
        def _():
            forward(s + 1)

        drain(xs.at[s, 1 - core], far.at[s])
        x_s = standardize(xs[s]).reshape(N * B, C).astype(BF)
        k = jnp.dot(x_s, w_in[:, C : 2 * C], preferred_element_type=F32).astype(BF)
        v = jnp.dot(x_s, w_in[:, 2 * C : 3 * C], preferred_element_type=F32).astype(BF)
        q_s = q_all[s]
        q_h = jnp.concatenate([jnp.where(head == h, q_s, 0.0) for h in range(H)], 0).astype(BF)
        scores = lax.dot_general(
            q_h, k, (((1,), (1,)), ((), ())), preferred_element_type=F32
        ) + bias[...].reshape(H * B, N * B)
        e = jnp.exp(scores - jnp.max(scores, -1, keepdims=True))
        att = jnp.dot(e.astype(BF), v, preferred_element_type=F32)
        att = (att / jnp.sum(e, -1, keepdims=True)).reshape(H, B, C)
        total = jnp.where(head == 0, att[0], 0.0)
        for h in range(1, H):
            total = jnp.where(head == h, att[h], total)
        gated = (gates[s] * total).astype(BF)
        x_new[s] = (
            x[s].astype(F32) + jnp.dot(gated, w_out[...], preferred_element_type=F32)
        ).astype(BF)

    for g in range(7):
        drain(x, sem.at[2])
    drain(xs.at[:, 0], sem.at[3])


def spread(block, out, B):
    blocks = [block(k) for k in range(N)]
    for i in range(B):
        out[:, i, :] = jnp.concatenate([b[:, i * B : (i + 1) * B] for b in blocks], 1)


def outer_body(
    x_new, pair, w_sides, w_outer, w_tri, got, mid, gate,
    flat, left, right, chunk, lefts, rights, left_s, right_s, tall, stacked, w_wide, normed,
    left_edge, right_edge, sem,
):
    r, c = here()
    core = lax.rem(c, 2)
    mate = c + 1 - 2 * core
    mine = c // 2
    parity = lax.rem(r, 2)
    S, B, C = x_new.shape
    O = w_sides.shape[0] // 2
    Z = pair.shape[2]
    G = B // 4
    for s in range(1, N):
        greet((lax.rem(r + s, N), c))
    for s in range(1, N):
        greet((r, lax.rem(c + s, N)))
    for s in range(8):
        k = 2 * lax.rem(mine + s, 8) + core

        @pl.when((k != r) | (r != c))
        def _():
            greet((k, r))

    flat[:, : 2 * O] = lax.dot_general(
        standardize(x_new[...]).astype(BF).reshape(S * B, C), w_sides[...],
        (((1,), (1,)), ((), ())), preferred_element_type=F32,
    )
    for k, side in ((0, left), (O, right)):
        lanes = jnp.concatenate(
            [flat[pl.ds(u, S * G, stride=4), :][:, k : k + O] for u in range(4)], 1
        )
        for s in range(S):
            side[s] = lanes[s * G : (s + 1) * G].astype(BF)
    greeted(38 - jnp.where(r == c, 1, 0))
    for s in range(8):
        g = lax.rem(r // 2 + s, 8)
        k = 2 * g + parity
        own = (k == c) & (r == c)

        @pl.when(jnp.logical_not(own))
        def _():
            push(left.at[g], chunk.at[r // 2], sem.at[0], sem.at[1], (c, k))

        @pl.when(own)
        def _():
            local(left.at[g], chunk.at[r // 2], sem.at[1])

    for s in range(1, N):
        push(right, rights.at[parity, :, r // 2], sem.at[2], sem.at[3], (lax.rem(r + s, N), c))
    local(right, rights.at[parity, :, r // 2], sem.at[3])
    drain(chunk, sem.at[1])
    for s in range(1, 8):
        push(chunk, lefts.at[core, mine], sem.at[6], sem.at[7], (r, lax.rem(c + 2 * s, N)))
    local(chunk, lefts.at[core, mine], sem.at[7])

    w_wide[...] = jnp.zeros_like(w_wide)
    tall[pl.ds(0, O * O), :] = w_outer[...].astype(F32)
    for d in range(O):
        part = tall[pl.ds(d, O, stride=O), :].astype(BF)
        for i in range(4):
            w_wide[pl.ds(d * 4 * O + i * O, O), i * Z : (i + 1) * Z] = part
    drain(lefts.at[core], sem.at[7])
    push(lefts.at[core], lefts.at[core], sem.at[8], sem.at[9], (r, mate))
    drain(chunk.at[pl.ds(0, 7)], sem.at[0])

    @pl.when(r != c)
    def _():
        drain(chunk.at[0], sem.at[0])

    for s in range(N - 1):
        drain(right, sem.at[2])
    drain(lefts.at[0, pl.ds(0, 7)], sem.at[6])
    drain(rights, sem.at[3])
    right_s[...] = rights[...].astype(F32).reshape(S * N, G, 4 * O)
    for k in range(G):
        tall[pl.ds(k * 4 * O, 4 * O), :] = right_s[:, k, :].T
    right_t = jnp.concatenate([tall[pl.ds(d, B, stride=O), :] for d in range(O)], 0).astype(BF)
    drain(lefts.at[0], sem.at[8])
    drain(lefts.at[1 - core], sem.at[9])
    left_s[...] = lefts[...].astype(F32).reshape(S * N, G, 4 * O)
    for g in range(B // 8):
        halves = [
            jnp.dot(right_t, left_s[:, k, :].astype(BF), preferred_element_type=F32)
            * (1.0 / (S * N))
            for k in (2 * g, 2 * g + 1)
        ]
        for d in range(O):
            stacked[pl.ds(g * 2 * B, 2 * B), d * 4 * O : (d + 1) * 4 * O] = jnp.concatenate(
                [h[d * B : (d + 1) * B] for h in halves], 0
            ).astype(BF)
    wide = jnp.dot(stacked[...], w_wide[...], preferred_element_type=F32)
    for i in range(B):
        k, u = i // 4, i % 4
        row = (pair[i].astype(F32) + wide[k * B : (k + 1) * B, u * Z : (u + 1) * Z]).astype(BF)
        mid[i] = row
        normed[pl.ds(i * B, B), :] = standardize(row)
    tri_n = normed[...].astype(BF)

    def edge(k):
        w = w_tri[:, 2 * k * Z : 2 * (k + 1) * Z]
        both = lax.dot_general(w, tri_n, (((0,), (1,)), ((), ())), preferred_element_type=F32)
        return (jax.nn.sigmoid(both[Z:]) * both[:Z]).astype(BF).reshape(8, N, B * B)

    for k, ref in ((0, left_edge), (1, right_edge)):
        ref[...] = edge(k)
        for s in range(8):
            g = lax.rem(c // 2 + s, 8)
            to = 2 * g + lax.rem(parity + 1 + k, 2)
            if s == 0:

                @pl.when(to != c)
                def _():
                    push(ref.at[g], got.at[c], sem.at[4], sem.at[5], (r, to))

                @pl.when(to == c)
                def _():
                    local(ref.at[g], got.at[c], sem.at[5])
            else:
                push(ref.at[g], got.at[c], sem.at[4], sem.at[5], (r, to))
    gate[...] = jax.nn.sigmoid(jnp.dot(tri_n, w_tri[:, 4 * Z :], preferred_element_type=F32))
    drain(got.at[pl.ds(0, N - 1)], sem.at[4])
    drain(got, sem.at[5])


def triangle_body(
    edges, mid, gate, w, out, spreads, parts, got, mates, sums, channel, back, flat, tiles, sem
):
    r, c = here()
    core = lax.rem(c, 2)
    mate = c + 1 - 2 * core
    mine = c // 2
    B = mid.shape[0]
    Z = mid.shape[2]
    R = N * B
    kind = lax.rem(r + core, 2)
    for s in range(1, N):
        greet((lax.rem(r + s, N), c))
    greet((r, mate))
    for s in range(1, 8):
        greet((r, lax.rem(c + 2 * s, N)))
    for h in range(2):
        spread(lambda k: edges[k].astype(F32)[8 * h : 8 * h + 8], spreads, B)
        parts[pl.ds(8 * h, 8)] = spreads[...].astype(BF)
        if h == 0:
            greeted(23)
        arrived = sem.at[1 + lax.rem(r, 2)]
        for s in range(8):
            q = 8 * h + lax.rem(r + s, 8)
            if s == 0:

                @pl.when(q != r)
                def _():
                    push(parts.at[q], got.at[kind, r // 2], sem.at[0], arrived, (q, c))

                @pl.when(q == r)
                def _():
                    local(parts.at[q], got.at[kind, r // 2], arrived)
            else:
                push(parts.at[q], got.at[kind, r // 2], sem.at[0], arrived, (q, c))
    drain(got.at[1], sem.at[2 - core])
    push(got.at[1], mates, sem.at[3], sem.at[4], (r, mate))
    drain(got.at[0], sem.at[1 + core])
    columns = got[0].reshape(8 * B, R)
    for rows, parity in ((got.at[1], 1 - core), (mates, core)):
        if rows is mates:
            drain(mates, sem.at[4])
        total = lax.dot_general(
            rows[...].reshape(8 * B, R), columns, (((1,), (1,)), ((), ())), preferred_element_type=F32
        )
        for s in range(8):
            q = 2 * s + parity
            sums[q] = total[s * B : (s + 1) * B].astype(BF)

            @pl.when(q != r)
            def _():
                push(sums.at[q], channel.at[r], sem.at[5], sem.at[6], (q, c))

            @pl.when(q == r)
            def _():
                local(sums.at[q], channel.at[r], sem.at[6])
    drain(parts.at[pl.ds(0, N - 1)], sem.at[0])
    drain(mates, sem.at[3])
    drain(sums.at[pl.ds(0, N - 1)], sem.at[5])
    drain(channel, sem.at[6])
    back[...] = channel[...].astype(F32)
    rows = [back[:, i, :] for i in range(B)]
    for g in range(8):
        flat[g] = jnp.concatenate([v[:, g * B : (g + 1) * B] for v in rows], 1).astype(BF)
    for s in range(1, 8):
        g = lax.rem(mine + s, 8)
        push(flat.at[g], tiles.at[mine], sem.at[7], sem.at[8], (r, 2 * g + core))
    local(flat.at[mine], tiles.at[mine], sem.at[8])
    drain(flat.at[pl.ds(0, 7)], sem.at[7])
    drain(tiles, sem.at[8])
    tri_ln = standardize(tiles[...].reshape(Z, B * B), 0).astype(BF)
    update = lax.dot_general(
        tri_ln, w[...], (((0,), (0,)), ((), ())), preferred_element_type=F32
    )
    out[...] = (mid[...].astype(F32) + (gate[...] * update).reshape(B, B, Z)).astype(BF)


def like(shape, dtype=BF):
    return jax.ShapeDtypeStruct(shape, dtype)


def shards(x, pair, w_in, w_out, w_bias, w_sides, w_outer, w_tri, w_tri_out):
    core = lax.rem(lax.axis_index("col"), 2)
    S, B, C = x.shape
    Z = pair.shape[2]
    H = w_bias.shape[1]
    O = w_sides.shape[1] // 2
    G = B // 4
    SP = S * N
    R = B * N

    VM = pltpu.VMEM
    x_new = comm_call(
        attention_body, "attention", 1, like((S, B, C)), [x, pair, w_in, w_out, w_bias.T], 4,
        [VM((S, 2, 8, B, C), BF), VM((H, B * B), BF), VM((N, H, B * B), BF), VM((H, B, R), F32),
         VM((S, B, C), F32), VM((S, B, C), F32),
         pltpu.SemaphoreType.DMA((S,)), pltpu.SemaphoreType.DMA((S,))],
    )
    edges, mid, gate = comm_call(
        outer_body, "outer", 2,
        [like((N, N, B * B)), like((B, B, Z)), like((B * B, Z), F32)],
        [x_new, pair, w_sides.T, w_outer, w_tri], 10,
        [VM((S * B, 128), F32), VM((S, G, 4 * O), BF), VM((S, G, 4 * O), BF), VM((8, G, 4 * O), BF),
         VM((2, S, 8, G, 4 * O), BF), VM((2, S, 8, G, 4 * O), BF), VM((SP, G, 4 * O), F32),
         VM((SP, G, 4 * O), F32), VM((B * O, SP), F32), VM((10 * B, 4 * O * O), BF),
         VM((4 * O * O, 4 * Z), BF), VM((B * B, Z), F32), VM((8, N, B * B), BF), VM((8, N, B * B), BF)],
    )
    pair_new = comm_call(
        triangle_body, "triangle", 3, like((B, B, Z)), [edges, mid, gate, w_tri_out], 9,
        [VM((8, B, R), F32), VM((N, B, R), BF), VM((2, 8, B, R), BF), VM((8, B, R), BF),
         VM((N, B, 8 * B), BF), VM((N, B, 8 * B), BF), VM((N, B, 8 * B), F32), VM((8, N, B * B), BF),
         VM((8, N, B * B), BF)],
    )
    return x_new, pair_new


def solution(mesh):
    tile = P("row", "col", None)
    return jax.shard_map(
        shards,
        mesh=mesh,
        in_specs=(tile, tile) + (P(),) * 7,
        out_specs=(tile, tile),
        check_vma=False,
    )
```

```python
import functools

import jax
import jax.numpy as jnp
from jax import lax
from jax.experimental import pallas as pl
from jax.experimental.pallas import tpu as pltpu
from jax.sharding import PartitionSpec

MESH = pl.DeviceIdType.MESH
EPS = 1e-05
N = 16
BF = jnp.bfloat16
F32 = jnp.float32


def standardize(v, axis=-1):
    v = v.astype(F32)
    center = v - jnp.mean(v, axis=axis, keepdims=True)
    spread = jnp.mean(center * center, axis=axis, keepdims=True)
    return center * lax.rsqrt(spread + EPS)


def here():
    return lax.axis_index("row"), lax.axis_index("col")


def push(src, dst, send, recv, to):
    pltpu.make_async_remote_copy(src, dst, send, recv, device_id=to, device_id_type=MESH).start()


def local(src, dst, recv):
    pltpu.make_async_copy(src, dst, recv).start()


def drain(ref, sem):
    pltpu.make_async_copy(ref, ref, sem).wait()


def greet(to):
    pl.semaphore_signal(pltpu.get_barrier_semaphore(), inc=1, device_id=to, device_id_type=MESH)


def greeted(count):
    pl.semaphore_wait(pltpu.get_barrier_semaphore(), count)


def comm_call(body, name, collective_id, outs, ins, sems, scratch=(), place=pltpu.VMEM):
    return pl.pallas_call(
        body,
        name=name,
        out_shape=outs,
        in_specs=[pl.BlockSpec(memory_space=place)] * len(ins),
        out_specs=[pl.BlockSpec(memory_space=place)] * len(outs),
        scratch_shapes=[*scratch, pltpu.SemaphoreType.DMA((sems,))],
        compiler_params=pltpu.CompilerParams(
            collective_id=collective_id, has_side_effects=True, vmem_limit_bytes=62 << 20
        ),
    )(*ins)


def block_body(
    x_in, pair_in, w_in_in, w_out_in, w_bias_in, w_sides_in, w_outer_in, w_tri_in, w_last_in,
    x_out, pair_out,
    x, pair, w_in, w_out, w_bias, w_sides, w_outer, w_tri, w_last,
    x_new, got, mid, gate, pair_new, xs, bias_out, bias_in, biases, bias, q_all, gates, v_all, scores_all, gated,
    flat, left, right, chunk, lefts, rights, left_s, right_s, tall, stacked, w_wide, normed,
    left_edge, right_edge, spreads, parts, held, mates, sums, channel, back, outgoing, tiles,
    near, far, load, back_sem, sem,
):
    r, c = here()
    core = lax.rem(c, 2)
    mate = c + 1 - 2 * core
    mine = c // 2
    parity = lax.rem(r, 2)
    S, B, C = x.shape
    H = w_bias.shape[0]
    D = C // H
    O = w_sides.shape[0] // 2
    Z = pair.shape[2]
    G = B // 4
    P = bias_out.shape[0]
    loads = [
        pltpu.make_async_copy(src, dst, load.at[k])
        for k, (src, dst) in enumerate(
            (
                (pair_in, pair), (w_bias_in, w_bias), (x_in, x), (w_in_in, w_in), (w_out_in, w_out),
                (w_sides_in, w_sides), (w_outer_in, w_outer), (w_tri_in, w_tri),
                (w_last_in, w_last),
            )
        )
    ]
    for cp in loads:
        cp.start()
    for s in range(1, N):
        greet((r, lax.rem(c + s, N)))
    for s in range(1, N):
        greet((lax.rem(r + s, N), c))

    @pl.when(r < P)
    def _():
        for s in range(N):
            k = lax.rem(c + s, N)

            @pl.when((c != r) | (k != c))
            def _():
                greet((c, k))

    for s in range(8):
        k = 2 * lax.rem(mine + s, 8) + core

        @pl.when((k != r) | (r != c))
        def _():
            greet((k, r))

    loads[0].wait()
    loads[1].wait()
    pair_n = standardize(pair[...]).astype(BF).reshape(B * B, Z)
    bias_flat = lax.dot_general(
        w_bias[...], pair_n, (((1,), (1,)), ((), ())), preferred_element_type=F32
    )
    bias_flat = jnp.concatenate([bias_flat, jnp.zeros((H, P * 128 - B * B), F32)], 1).astype(BF)
    for k in range(P):
        bias_out[k] = bias_flat[:, k * 128 : (k + 1) * 128]
    own_p = (r == c) & (r < P)
    greeted(38 + P - jnp.where(r == c, 1, 0) - jnp.where(own_p, 1, 0))
    for s in range(P):
        k = lax.rem(s + c, P)
        own = (k == r) & (r == c)

        @pl.when(jnp.logical_not(own))
        def _():
            push(bias_out.at[k], bias_in.at[c], sem.at[10], sem.at[11], (k, r))

        @pl.when(own)
        def _():
            local(bias_out.at[k], bias_in.at[c], sem.at[11])

    @pl.loop(0, S)
    def _(s):
        for g in range(1, 8):
            push(x_in.at[s], xs.at[s, core, mine], sem.at[12], near.at[s], (r, lax.rem(c + 2 * g, N)))
        local(x_in.at[s], xs.at[s, core, mine], near.at[s])

    @pl.when(r < P)
    def _():
        drain(bias_in, sem.at[11])
        for s in range(1, N):
            push(bias_in, biases.at[r], sem.at[4], sem.at[5], (lax.rem(r + s, N), c))
        local(bias_in, biases.at[r], sem.at[5])

    def forward(s):
        drain(xs.at[s, core], near.at[s])
        push(xs.at[s, core], xs.at[s, core], sem.at[13], far.at[s], (r, mate))

    for cp in loads[2:]:
        cp.wait()
    own_n = standardize(x[...]).astype(BF).reshape(S * B, C)
    q = jnp.dot(own_n, w_in[:, :C], preferred_element_type=F32) * D ** (-0.5)
    q_all[...] = q.reshape(S, B, C)
    gates[...] = jax.nn.sigmoid(jnp.dot(own_n, w_in[:, 3 * C :], preferred_element_type=F32))
    w_wide[...] = jnp.zeros_like(w_wide)
    tall[pl.ds(0, O * O), :] = w_outer[...].astype(F32)
    for d in range(O):
        part = tall[pl.ds(d, O, stride=O), :].astype(BF)
        for i in range(4):
            w_wide[pl.ds(d * 4 * O + i * O, O), i * Z : (i + 1) * Z] = part
    head = lax.broadcasted_iota(jnp.int32, (B, C), 1) // D
    forward(0)

    @pl.loop(0, S)
    def _(s):
        @pl.when(s < S - 1)
        def _():
            forward(s + 1)

        drain(xs.at[s, 1 - core], far.at[s])
        x_s = standardize(xs[s]).reshape(N * B, C).astype(BF)
        k = jnp.dot(x_s, w_in[:, C : 2 * C], preferred_element_type=F32).astype(BF)
        v_all[s] = jnp.dot(x_s, w_in[:, 2 * C : 3 * C], preferred_element_type=F32).astype(BF)
        q_s = q_all[s]
        q_h = jnp.concatenate([jnp.where(head == h, q_s, 0.0) for h in range(H)], 0).astype(BF)
        scores_all[s] = lax.dot_general(
            q_h, k, (((1,), (1,)), ((), ())), preferred_element_type=F32
        )

    drain(bias_out.at[pl.ds(0, P - 1)], sem.at[10])

    @pl.when(jnp.logical_not(own_p))
    def _():
        drain(bias_out.at[0], sem.at[10])

    @pl.when(r < P)
    def _():
        for s in range(1, N):
            drain(bias_in, sem.at[4])

    drain(biases, sem.at[5])

    def bias_of(k):
        block = 2 * (k % 8) + k // 8
        return jnp.concatenate([biases[p, block].astype(F32) for p in range(P)], 1)

    spread(bias_of, bias, B)
    for half in range(2):
        first, count = half * S // 2, S // 2

        @pl.loop(first, first + count)
        def _(s):
            scores = scores_all[s] + bias[...].reshape(H * B, N * B)
            e = jnp.exp(scores - jnp.max(scores, -1, keepdims=True))
            att = jnp.dot(e.astype(BF), v_all[s], preferred_element_type=F32)
            att = (att / jnp.sum(e, -1, keepdims=True)).reshape(H, B, C)
            total = jnp.where(head == 0, att[0], 0.0)
            for h in range(1, H):
                total = jnp.where(head == h, att[h], total)
            gated[pl.ds(pl.multiple_of(s * B, 8), B), :] = total

        span = slice(first * B, (first + count) * B)
        update = jnp.dot(
            (gated[span] * gates[span]).astype(BF), w_out[...], preferred_element_type=F32
        )
        x_half = (
            x[first : first + count].astype(F32) + update.reshape(count, B, C)
        ).astype(BF)
        x_new[first : first + count] = x_half
        flat[span, : 2 * O] = lax.dot_general(
            standardize(x_half).astype(BF).reshape(count * B, C), w_sides[...],
            (((1,), (1,)), ((), ())), preferred_element_type=F32,
        )
        for k, side in ((0, left), (O, right)):
            lanes = jnp.concatenate(
                [flat[pl.ds(first * B + u, count * G, stride=4), :][:, k : k + O] for u in range(4)], 1
            )
            for s in range(count):
                side[first + s] = lanes[s * G : (s + 1) * G].astype(BF)
        for s in range(first, first + count):
            k = 2 * s + parity
            own = (k == c) & (r == c)

            @pl.when(jnp.logical_not(own))
            def _():
                push(left.at[s], chunk.at[r // 2], sem.at[0], sem.at[1], (c, k))

            @pl.when(own)
            def _():
                local(left.at[s], chunk.at[r // 2], sem.at[1])

        part = right.at[pl.ds(first, count)]
        there = rights.at[parity, pl.ds(first, count), r // 2]
        for s in range(1, N):
            push(part, there, sem.at[2], sem.at[3], (lax.rem(r + s, N), c))
        local(part, there, sem.at[3])
    x_done = pltpu.make_async_copy(x_new, x_out, load.at[0])
    x_done.start()
    drain(chunk, sem.at[1])
    for s in range(1, 8):
        push(chunk, lefts.at[core, mine], sem.at[6], sem.at[7], (r, lax.rem(c + 2 * s, N)))
    local(chunk, lefts.at[core, mine], sem.at[7])
    for g in range(7):
        drain(xs.at[:, 0, 0], sem.at[12])
    drain(xs.at[:, 0], sem.at[13])
    drain(lefts.at[core], sem.at[7])
    push(lefts.at[core], lefts.at[core], sem.at[8], sem.at[9], (r, mate))
    drain(chunk.at[pl.ds(0, 7)], sem.at[0])

    @pl.when(r != c)
    def _():
        drain(chunk.at[0], sem.at[0])

    for s in range(N - 1):
        drain(right, sem.at[2])
    drain(lefts.at[0, pl.ds(0, 7)], sem.at[6])
    drain(rights, sem.at[3])
    right_s[...] = rights[...].astype(F32).reshape(S * N, G, 4 * O)
    for k in range(G):
        tall[pl.ds(k * 4 * O, 4 * O), :] = right_s[:, k, :].T
    right_t = jnp.concatenate([tall[pl.ds(d, B, stride=O), :] for d in range(O)], 0).astype(BF)
    drain(lefts.at[0], sem.at[8])
    drain(lefts.at[1 - core], sem.at[9])
    left_s[...] = lefts[...].astype(F32).reshape(S * N, G, 4 * O)
    for g in range(B // 8):
        halves = [
            jnp.dot(right_t, left_s[:, k, :].astype(BF), preferred_element_type=F32)
            * (1.0 / (S * N))
            for k in (2 * g, 2 * g + 1)
        ]
        for d in range(O):
            stacked[pl.ds(g * 2 * B, 2 * B), d * 4 * O : (d + 1) * 4 * O] = jnp.concatenate(
                [h[d * B : (d + 1) * B] for h in halves], 0
            ).astype(BF)
    wide = jnp.dot(stacked[...], w_wide[...], preferred_element_type=F32)
    for i in range(B):
        k, u = i // 4, i % 4
        row = (pair[i].astype(F32) + wide[k * B : (k + 1) * B, u * Z : (u + 1) * Z]).astype(BF)
        mid[i] = row
        normed[pl.ds(i * B, B), :] = standardize(row)
    tri_n = normed[...].astype(BF)

    def edge(k):
        w = w_tri[:, 2 * k * Z : 2 * (k + 1) * Z]
        both = lax.dot_general(w, tri_n, (((0,), (1,)), ((), ())), preferred_element_type=F32)
        return (jax.nn.sigmoid(both[Z:]) * both[:Z]).astype(BF).reshape(8, N, B * B)

    for k, ref in ((0, left_edge), (1, right_edge)):
        ref[...] = edge(k)
        for s in range(8):
            g = lax.rem(c // 2 + s, 8)
            to = 2 * g + lax.rem(parity + 1 + k, 2)
            if s == 0:

                @pl.when(to != c)
                def _():
                    push(ref.at[g], got.at[c], sem.at[14], sem.at[15], (r, to))

                @pl.when(to == c)
                def _():
                    local(ref.at[g], got.at[c], sem.at[15])
            else:
                push(ref.at[g], got.at[c], sem.at[14], sem.at[15], (r, to))
    gate[...] = jax.nn.sigmoid(jnp.dot(tri_n, w_tri[:, 4 * Z :], preferred_element_type=F32))
    drain(got.at[pl.ds(0, N - 1)], sem.at[14])
    drain(got, sem.at[15])
    kind = lax.rem(r + core, 2)
    R = N * B
    for h in range(2):
        spread(lambda k: got[k].astype(F32)[8 * h : 8 * h + 8], spreads, B)
        parts[pl.ds(8 * h, 8)] = spreads[...].astype(BF)
        arrived = back_sem.at[1 + lax.rem(r, 2)]
        for s in range(8):
            q = 8 * h + lax.rem(r + s, 8)
            if s == 0:

                @pl.when(q != r)
                def _():
                    push(parts.at[q], held.at[kind, r // 2], back_sem.at[0], arrived, (q, c))

                @pl.when(q == r)
                def _():
                    local(parts.at[q], held.at[kind, r // 2], arrived)
            else:
                push(parts.at[q], held.at[kind, r // 2], back_sem.at[0], arrived, (q, c))
    drain(held.at[1], back_sem.at[2 - core])
    push(held.at[1], mates, back_sem.at[3], back_sem.at[4], (r, mate))
    drain(held.at[0], back_sem.at[1 + core])
    columns = held[0].reshape(8 * B, R)
    for rows, parity in ((held.at[1], 1 - core), (mates, core)):
        if rows is mates:
            drain(mates, back_sem.at[4])
        total = lax.dot_general(
            rows[...].reshape(8 * B, R), columns, (((1,), (1,)), ((), ())), preferred_element_type=F32
        )
        for s in range(8):
            q = 2 * s + parity
            sums[q] = total[s * B : (s + 1) * B].astype(BF)

            @pl.when(q != r)
            def _():
                push(sums.at[q], channel.at[r], back_sem.at[5], back_sem.at[6], (q, c))

            @pl.when(q == r)
            def _():
                local(sums.at[q], channel.at[r], back_sem.at[6])
    drain(parts.at[pl.ds(0, N - 1)], back_sem.at[0])
    drain(mates, back_sem.at[3])
    drain(sums.at[pl.ds(0, N - 1)], back_sem.at[5])
    drain(channel, back_sem.at[6])
    back[...] = channel[...].astype(F32)
    rows = [back[:, i, :] for i in range(B)]
    for g in range(8):
        outgoing[g] = jnp.concatenate([v[:, g * B : (g + 1) * B] for v in rows], 1).astype(BF)
    for s in range(1, 8):
        g = lax.rem(mine + s, 8)
        push(outgoing.at[g], tiles.at[mine], back_sem.at[7], back_sem.at[8], (r, 2 * g + core))
    local(outgoing.at[mine], tiles.at[mine], back_sem.at[8])
    drain(outgoing.at[pl.ds(0, 7)], back_sem.at[7])
    drain(tiles, back_sem.at[8])
    tri_ln = standardize(tiles[...].reshape(Z, B * B), 0).astype(BF)
    update = lax.dot_general(
        tri_ln, w_last[...], (((0,), (0,)), ((), ())), preferred_element_type=F32
    )
    pair_new[...] = (mid[...].astype(F32) + (gate[...] * update).reshape(B, B, Z)).astype(BF)
    done = pltpu.make_async_copy(pair_new, pair_out, back_sem.at[9])
    done.start()
    done.wait()
    x_done.wait()


def spread(block, out, B):
    blocks = [block(k) for k in range(N)]
    for i in range(B):
        out[:, i, :] = jnp.concatenate([b[:, i * B : (i + 1) * B] for b in blocks], 1)


def like(shape, dtype=BF):
    return jax.ShapeDtypeStruct(shape, dtype)


def shards(x, pair, w_in, w_out, w_bias, w_sides, w_outer, w_tri, w_tri_out):
    core = lax.rem(lax.axis_index("col"), 2)
    S, B, C = x.shape
    Z = pair.shape[2]
    H = w_bias.shape[1]
    O = w_sides.shape[1] // 2
    G = B // 4
    SP = S * N
    R = B * N
    P = -(-B * B // 128)

    VM = pltpu.VMEM
    args = [x, pair, w_in, w_out, w_bias.T, w_sides.T, w_outer, w_tri, w_tri_out]
    return comm_call(
        block_body, "block", 1, [like((S, B, C)), like((B, B, Z))], args, 16,
        [*(VM(v.shape, BF) for v in args),
         VM((S, B, C), BF), VM((N, N, B * B), BF), VM((B, B, Z), BF), VM((B * B, Z), F32), VM((B, B, Z), BF),
         VM((S, 2, 8, B, C), BF), VM((P, H, 128), BF), VM((N, H, 128), BF), VM((P, N, H, 128), BF), VM((H, B, R), F32),
         VM((S, B, C), F32), VM((S * B, C), F32), VM((S, R, C), BF), VM((S, H * B, R), F32),
         VM((S * B, C), F32),
         VM((S * B, 128), F32), VM((S, G, 4 * O), BF), VM((S, G, 4 * O), BF), VM((8, G, 4 * O), BF),
         VM((2, S, 8, G, 4 * O), BF), VM((2, S, 8, G, 4 * O), BF), VM((SP, G, 4 * O), F32),
         VM((SP, G, 4 * O), F32), VM((B * O, SP), F32), VM((10 * B, 4 * O * O), BF),
         VM((4 * O * O, 4 * Z), BF), VM((B * B, Z), F32), VM((8, N, B * B), BF), VM((8, N, B * B), BF),
         VM((8, B, R), F32), VM((N, B, R), BF), VM((2, 8, B, R), BF), VM((8, B, R), BF),
         VM((N, B, 8 * B), BF), VM((N, B, 8 * B), BF), VM((N, B, 8 * B), F32), VM((8, N, B * B), BF),
         VM((8, N, B * B), BF),
         pltpu.SemaphoreType.DMA((S,)), pltpu.SemaphoreType.DMA((S,)), pltpu.SemaphoreType.DMA((9,)),
         pltpu.SemaphoreType.DMA((10,))],
        pltpu.HBM,
    )


def solution(mesh):
    tile = PartitionSpec("row", "col", None)
    return jax.shard_map(
        shards,
        mesh=mesh,
        in_specs=(tile, tile) + (PartitionSpec(),) * 7,
        out_specs=(tile, tile),
        check_vma=False,
    )
```

```python
import functools

import jax
import jax.numpy as jnp
from jax import lax
from jax.experimental import pallas as pl
from jax.experimental.pallas import tpu as pltpu
from jax.sharding import PartitionSpec

MESH = pl.DeviceIdType.MESH
EPS = 1e-05
N = 16
AROUND = (1, 7, 2, 6, 3, 5, 4, 0)
AROUND_16 = (1, 15, 2, 14, 3, 13, 4, 12, 5, 11, 6, 10, 7, 9, 8)
BF = jnp.bfloat16
F32 = jnp.float32


def standardize(v, axis=-1):
    v = v.astype(F32)
    center = v - jnp.mean(v, axis=axis, keepdims=True)
    spread = jnp.mean(center * center, axis=axis, keepdims=True)
    return center * lax.rsqrt(spread + EPS)


def here():
    return lax.axis_index("row"), lax.axis_index("col")


def push(src, dst, send, recv, to):
    pltpu.make_async_remote_copy(src, dst, send, recv, device_id=to, device_id_type=MESH).start()


def local(src, dst, recv):
    pltpu.make_async_copy(src, dst, recv).start()


def drain(ref, sem):
    pltpu.make_async_copy(ref, ref, sem).wait()


def greet(to):
    pl.semaphore_signal(pltpu.get_barrier_semaphore(), inc=1, device_id=to, device_id_type=MESH)


def greeted(count):
    pl.semaphore_wait(pltpu.get_barrier_semaphore(), count)


def comm_call(body, name, collective_id, outs, ins, sems, scratch=(), place=pltpu.VMEM):
    return pl.pallas_call(
        body,
        name=name,
        out_shape=outs,
        in_specs=[pl.BlockSpec(memory_space=place)] * len(ins),
        out_specs=[pl.BlockSpec(memory_space=place)] * len(outs),
        scratch_shapes=[*scratch, pltpu.SemaphoreType.DMA((sems,))],
        compiler_params=pltpu.CompilerParams(
            collective_id=collective_id, has_side_effects=True, vmem_limit_bytes=62 << 20
        ),
    )(*ins)


def block_body(
    x_in, pair_in, w_in_in, w_out_in, w_bias_in, w_sides_in, w_outer_in, w_tri_in, w_last_in,
    x_out, pair_out,
    x, pair, w_in, w_out, w_bias, w_sides, w_outer, w_tri, w_last,
    x_new, got, mid, gate, pair_new, xs, bias_out, bias_in, biases, bias, q_all, gates, v_all, scores_all, gated,
    flat, left, right, chunk, lefts, rights, left_s, right_s, tall, stacked, w_wide, normed,
    left_edge, right_edge, spreads, parts, held, mates, sums_0, sums_1, channel_0, channel_1, back_0, back_1,
    outgoing_0, outgoing_1, tiles_0, tiles_1,
    near, far, load, back_sem, sem,
):
    sums, channel, back = (sums_0, sums_1), (channel_0, channel_1), (back_0, back_1)
    outgoing, tiles = (outgoing_0, outgoing_1), (tiles_0, tiles_1)
    r, c = here()
    core = lax.rem(c, 2)
    mate = c + 1 - 2 * core
    mine = c // 2
    parity = lax.rem(r, 2)
    S, B, C = x.shape
    H = w_bias.shape[0]
    D = C // H
    O = w_sides.shape[0] // 2
    Z = pair.shape[2]
    G = B // 4
    P = bias_out.shape[0]
    loads = [
        pltpu.make_async_copy(src, dst, load.at[k])
        for k, (src, dst) in enumerate(
            (
                (pair_in, pair), (w_bias_in, w_bias), (x_in, x), (w_in_in, w_in), (w_out_in, w_out),
                (w_sides_in, w_sides), (w_outer_in, w_outer), (w_tri_in, w_tri),
                (w_last_in, w_last),
            )
        )
    ]
    for cp in loads:
        cp.start()
    for s in range(1, N):
        greet((r, lax.rem(c + s, N)))
    for s in range(1, N):
        greet((lax.rem(r + s, N), c))

    @pl.when(r < P)
    def _():
        for s in range(N):
            k = lax.rem(c + s, N)

            @pl.when((c != r) | (k != c))
            def _():
                greet((c, k))

    for s in range(8):
        k = 2 * lax.rem(mine + s, 8) + core

        @pl.when((k != r) | (r != c))
        def _():
            greet((k, r))

    loads[0].wait()
    loads[1].wait()
    pair_n = standardize(pair[...]).astype(BF).reshape(B * B, Z)
    bias_flat = lax.dot_general(
        w_bias[...], pair_n, (((1,), (1,)), ((), ())), preferred_element_type=F32
    )
    bias_flat = jnp.concatenate([bias_flat, jnp.zeros((H, P * 128 - B * B), F32)], 1).astype(BF)
    for k in range(P):
        bias_out[k] = bias_flat[:, k * 128 : (k + 1) * 128]
    own_p = (r == c) & (r < P)
    greeted(38 + P - jnp.where(r == c, 1, 0) - jnp.where(own_p, 1, 0))
    for s in range(P):
        k = lax.rem(s + c, P)
        own = (k == r) & (r == c)

        @pl.when(jnp.logical_not(own))
        def _():
            push(bias_out.at[k], bias_in.at[c], sem.at[10], sem.at[11], (k, r))

        @pl.when(own)
        def _():
            local(bias_out.at[k], bias_in.at[c], sem.at[11])

    @pl.loop(0, S)
    def _(s):
        for g in AROUND[:-1]:
            push(x_in.at[s], xs.at[s, core, mine], sem.at[12], near.at[s], (r, lax.rem(c + 2 * g, N)))
        local(x_in.at[s], xs.at[s, core, mine], near.at[s])

    @pl.when(r < P)
    def _():
        drain(bias_in, sem.at[11])
        for s in AROUND_16:
            push(bias_in, biases.at[r], sem.at[4], sem.at[5], (lax.rem(r + s, N), c))
        local(bias_in, biases.at[r], sem.at[5])

    def forward(s):
        drain(xs.at[s, core], near.at[s])
        push(xs.at[s, core], xs.at[s, core], sem.at[13], far.at[s], (r, mate))

    for cp in loads[2:]:
        cp.wait()
    own_n = standardize(x[...]).astype(BF).reshape(S * B, C)
    q = jnp.dot(own_n, w_in[:, :C], preferred_element_type=F32) * D ** (-0.5)
    q_all[...] = q.reshape(S, B, C)
    gates[...] = jax.nn.sigmoid(jnp.dot(own_n, w_in[:, 3 * C :], preferred_element_type=F32))
    w_wide[...] = jnp.zeros_like(w_wide)
    tall[pl.ds(0, O * O), :] = w_outer[...].astype(F32)
    for d in range(O):
        part = tall[pl.ds(d, O, stride=O), :].astype(BF)
        for i in range(4):
            w_wide[pl.ds(d * 4 * O + i * O, O), i * Z : (i + 1) * Z] = part
    head = lax.broadcasted_iota(jnp.int32, (B, C), 1) // D
    forward(0)

    @pl.loop(0, S)
    def _(s):
        @pl.when(s < S - 1)
        def _():
            forward(s + 1)

        drain(xs.at[s, 1 - core], far.at[s])
        x_s = standardize(xs[s]).reshape(N * B, C).astype(BF)
        k = jnp.dot(x_s, w_in[:, C : 2 * C], preferred_element_type=F32).astype(BF)
        v_all[s] = jnp.dot(x_s, w_in[:, 2 * C : 3 * C], preferred_element_type=F32).astype(BF)
        q_s = q_all[s]
        q_h = jnp.concatenate([jnp.where(head == h, q_s, 0.0) for h in range(H)], 0).astype(BF)
        scores_all[s] = lax.dot_general(
            q_h, k, (((1,), (1,)), ((), ())), preferred_element_type=F32
        )

    drain(bias_out.at[pl.ds(0, P - 1)], sem.at[10])

    @pl.when(jnp.logical_not(own_p))
    def _():
        drain(bias_out.at[0], sem.at[10])

    @pl.when(r < P)
    def _():
        for s in range(1, N):
            drain(bias_in, sem.at[4])

    drain(biases, sem.at[5])

    def bias_of(k):
        block = 2 * (k % 8) + k // 8
        return jnp.concatenate([biases[p, block].astype(F32) for p in range(P)], 1)

    spread(bias_of, bias, B)
    for half in range(2):
        first, count = half * S // 2, S // 2

        @pl.loop(first, first + count)
        def _(s):
            scores = scores_all[s] + bias[...].reshape(H * B, N * B)
            e = jnp.exp(scores - jnp.max(scores, -1, keepdims=True))
            att = jnp.dot(e.astype(BF), v_all[s], preferred_element_type=F32)
            att = (att / jnp.sum(e, -1, keepdims=True)).reshape(H, B, C)
            total = jnp.where(head == 0, att[0], 0.0)
            for h in range(1, H):
                total = jnp.where(head == h, att[h], total)
            gated[pl.ds(pl.multiple_of(s * B, 8), B), :] = total

        span = slice(first * B, (first + count) * B)
        update = jnp.dot(
            (gated[span] * gates[span]).astype(BF), w_out[...], preferred_element_type=F32
        )
        x_half = (
            x[first : first + count].astype(F32) + update.reshape(count, B, C)
        ).astype(BF)
        x_new[first : first + count] = x_half
        flat[span, : 2 * O] = lax.dot_general(
            standardize(x_half).astype(BF).reshape(count * B, C), w_sides[...],
            (((1,), (1,)), ((), ())), preferred_element_type=F32,
        )
        for k, side in ((0, left), (O, right)):
            lanes = jnp.concatenate(
                [flat[pl.ds(first * B + u, count * G, stride=4), :][:, k : k + O] for u in range(4)], 1
            )
            for s in range(count):
                side[first + s] = lanes[s * G : (s + 1) * G].astype(BF)
        for s in range(first, first + count):
            k = 2 * s + parity
            own = (k == c) & (r == c)

            @pl.when(jnp.logical_not(own))
            def _():
                push(left.at[s], chunk.at[r // 2], sem.at[0], sem.at[1], (c, k))

            @pl.when(own)
            def _():
                local(left.at[s], chunk.at[r // 2], sem.at[1])

        part = right.at[pl.ds(first, count)]
        there = rights.at[parity, pl.ds(first, count), r // 2]
        for s in AROUND_16:
            push(part, there, sem.at[2], sem.at[3], (lax.rem(r + s, N), c))
        local(part, there, sem.at[3])
    x_done = pltpu.make_async_copy(x_new, x_out, load.at[0])
    x_done.start()
    drain(chunk, sem.at[1])
    for s in AROUND[:-1]:
        push(chunk, lefts.at[core, mine], sem.at[6], sem.at[7], (r, lax.rem(c + 2 * s, N)))
    local(chunk, lefts.at[core, mine], sem.at[7])
    for g in range(7):
        drain(xs.at[:, 0, 0], sem.at[12])
    drain(xs.at[:, 0], sem.at[13])
    drain(lefts.at[core], sem.at[7])
    push(lefts.at[core], lefts.at[core], sem.at[8], sem.at[9], (r, mate))
    drain(chunk.at[pl.ds(0, 7)], sem.at[0])

    @pl.when(r != c)
    def _():
        drain(chunk.at[0], sem.at[0])

    for s in range(N - 1):
        drain(right, sem.at[2])
    drain(lefts.at[0, pl.ds(0, 7)], sem.at[6])
    drain(rights, sem.at[3])
    right_s[...] = rights[...].astype(F32).reshape(S * N, G, 4 * O)
    for k in range(G):
        tall[pl.ds(k * 4 * O, 4 * O), :] = right_s[:, k, :].T
    right_t = jnp.concatenate([tall[pl.ds(d, B, stride=O), :] for d in range(O)], 0).astype(BF)
    drain(lefts.at[0], sem.at[8])
    drain(lefts.at[1 - core], sem.at[9])
    left_s[...] = lefts[...].astype(F32).reshape(S * N, G, 4 * O)
    for g in range(B // 8):
        halves = [
            jnp.dot(right_t, left_s[:, k, :].astype(BF), preferred_element_type=F32)
            * (1.0 / (S * N))
            for k in (2 * g, 2 * g + 1)
        ]
        for d in range(O):
            stacked[pl.ds(g * 2 * B, 2 * B), d * 4 * O : (d + 1) * 4 * O] = jnp.concatenate(
                [h[d * B : (d + 1) * B] for h in halves], 0
            ).astype(BF)
    wide = jnp.dot(stacked[...], w_wide[...], preferred_element_type=F32)
    for i in range(B):
        k, u = i // 4, i % 4
        row = (pair[i].astype(F32) + wide[k * B : (k + 1) * B, u * Z : (u + 1) * Z]).astype(BF)
        mid[i] = row
        normed[pl.ds(i * B, B), :] = standardize(row)
    tri_n = normed[...].astype(BF)

    def edge(k):
        w = w_tri[:, 2 * k * Z : 2 * (k + 1) * Z]
        both = lax.dot_general(w, tri_n, (((0,), (1,)), ((), ())), preferred_element_type=F32)
        return (jax.nn.sigmoid(both[Z:]) * both[:Z]).reshape(8, 2, 8, B * B)

    def over_col(k, h):
        ref = (left_edge, right_edge)[k]
        for s in AROUND:
            g = lax.rem(mine + s, 8)
            to = 2 * g + lax.rem(parity + 1 + k, 2)
            if s == 0:

                @pl.when(to != c)
                def _():
                    push(ref.at[h, g], got.at[h, c], back_sem.at[14], back_sem.at[15 + h], (r, to))

                @pl.when(to == c)
                def _():
                    local(ref.at[h, g], got.at[h, c], back_sem.at[15 + h])
            else:
                push(ref.at[h, g], got.at[h, c], back_sem.at[14], back_sem.at[15 + h], (r, to))

    for k, ref in ((0, left_edge), (1, right_edge)):
        values = edge(k)
        for h in range(2):
            ref[h] = values[:, h].astype(BF)
        over_col(k, 0)
    over_col(0, 1)
    over_col(1, 1)
    gate[...] = jax.nn.sigmoid(jnp.dot(tri_n, w_tri[:, 4 * Z :], preferred_element_type=F32))
    kind = lax.rem(r + core, 2)
    R = N * B
    arrived = back_sem.at[1 + 2 * parity + r // 8]
    for h in range(2):
        drain(got.at[h], back_sem.at[15 + h])
        spread(lambda k: got[h, k].astype(F32), spreads, B)
        parts[pl.ds(8 * h, 8)] = spreads[...].astype(BF)
        for s in AROUND:
            q = 8 * h + lax.rem(r + s, 8)
            if s == 0:

                @pl.when(q != r)
                def _():
                    push(parts.at[q], held.at[kind, r // 2], back_sem.at[0], arrived, (q, c))

                @pl.when(q == r)
                def _():
                    local(parts.at[q], held.at[kind, r // 2], arrived)
            else:
                push(parts.at[q], held.at[kind, r // 2], back_sem.at[0], arrived, (q, c))
    for h in range(2):
        some = held.at[1, pl.ds(4 * h, 4)]
        drain(some, back_sem.at[3 - 2 * core + h])
        push(some, mates.at[pl.ds(4 * h, 4)], back_sem.at[5], back_sem.at[6], (r, mate))
    for h in range(2):
        drain(held.at[0, pl.ds(4 * h, 4)], back_sem.at[1 + 2 * core + h])
    columns = held[0].reshape(8 * B, R)
    rows = ((0, B * 3 // 5), (B * 3 // 5, B))

    def products(ref):
        return lax.dot_general(
            ref.reshape(8 * B, R), columns, (((1,), (1,)), ((), ())), preferred_element_type=F32
        )

    def over_row(piece, odd):
        for s in AROUND:
            q = 2 * lax.rem(r // 2 + s, 8) + odd

            @pl.when(q != r)
            def _():
                push(sums[piece].at[q], channel[piece].at[r], back_sem.at[7], back_sem.at[8 + piece], (q, c))

            @pl.when(q == r)
            def _():
                local(sums[piece].at[q], channel[piece].at[r], back_sem.at[8 + piece])

    for ref, odd in ((held.at[1], 1 - core), (mates, core)):
        if ref is mates:
            drain(mates, back_sem.at[6])
        total = products(ref[...])
        for piece, (low, high) in enumerate(rows):
            for s in range(8):
                sums[piece][2 * s + odd] = total[s * B + low : s * B + high].astype(BF)
            if piece == 0:
                over_row(0, odd)
    over_row(1, 1 - core)
    over_row(1, core)
    drain(parts.at[pl.ds(0, N - 1)], back_sem.at[0])
    drain(mates, back_sem.at[5])
    for piece in range(2):
        drain(channel[piece], back_sem.at[8 + piece])
        back[piece][...] = channel[piece][...].astype(F32)
        lines = [back[piece][:, i, :] for i in range(back[piece].shape[1])]
        for g in range(8):
            outgoing[piece][g] = jnp.concatenate([v[:, g * B : (g + 1) * B] for v in lines], 1).astype(BF)
        for s in AROUND[:-1]:
            g = lax.rem(mine + s, 8)
            push(
                outgoing[piece].at[g], tiles[piece].at[mine], back_sem.at[10], back_sem.at[11 + piece],
                (r, 2 * g + core),
            )
        local(outgoing[piece].at[mine], tiles[piece].at[mine], back_sem.at[11 + piece])
    for piece, (low, high) in enumerate(rows):
        drain(tiles[piece], back_sem.at[11 + piece])
        tri_ln = standardize(tiles[piece][...].reshape(Z, (high - low) * B), 0).astype(BF)
        update = lax.dot_general(
            tri_ln, w_last[...], (((0,), (0,)), ((), ())), preferred_element_type=F32
        )
        pair_new[low:high] = (
            mid[low:high].astype(F32)
            + (gate[low * B : high * B, :] * update).reshape(high - low, B, Z)
        ).astype(BF)
    for piece in range(2):
        drain(sums[piece].at[pl.ds(0, N - 1)], back_sem.at[7])
        drain(outgoing[piece].at[pl.ds(0, 7)], back_sem.at[10])
    for h in range(2):
        drain(got.at[h, pl.ds(0, N - 1)], back_sem.at[14])
    done = pltpu.make_async_copy(pair_new, pair_out, back_sem.at[13])
    done.start()
    done.wait()
    x_done.wait()


def spread(block, out, B):
    blocks = [block(k) for k in range(N)]
    for i in range(B):
        out[:, i, :] = jnp.concatenate([b[:, i * B : (i + 1) * B] for b in blocks], 1)


def like(shape, dtype=BF):
    return jax.ShapeDtypeStruct(shape, dtype)


def shards(x, pair, w_in, w_out, w_bias, w_sides, w_outer, w_tri, w_tri_out):
    core = lax.rem(lax.axis_index("col"), 2)
    S, B, C = x.shape
    Z = pair.shape[2]
    H = w_bias.shape[1]
    O = w_sides.shape[1] // 2
    G = B // 4
    SP = S * N
    R = B * N
    P = -(-B * B // 128)
    pieces = (B * 3 // 5, B - B * 3 // 5)

    VM = pltpu.VMEM
    args = [x, pair, w_in, w_out, w_bias.T, w_sides.T, w_outer, w_tri, w_tri_out]
    return comm_call(
        block_body, "block", 1, [like((S, B, C)), like((B, B, Z))], args, 16,
        [*(VM(v.shape, BF) for v in args),
         VM((S, B, C), BF), VM((2, N, 8, B * B), BF), VM((B, B, Z), BF), VM((B * B, Z), F32), VM((B, B, Z), BF),
         VM((S, 2, 8, B, C), BF), VM((P, H, 128), BF), VM((N, H, 128), BF), VM((P, N, H, 128), BF), VM((H, B, R), F32),
         VM((S, B, C), F32), VM((S * B, C), F32), VM((S, R, C), BF), VM((S, H * B, R), F32),
         VM((S * B, C), F32),
         VM((S * B, 128), F32), VM((S, G, 4 * O), BF), VM((S, G, 4 * O), BF), VM((8, G, 4 * O), BF),
         VM((2, S, 8, G, 4 * O), BF), VM((2, S, 8, G, 4 * O), BF), VM((SP, G, 4 * O), F32),
         VM((SP, G, 4 * O), F32), VM((B * O, SP), F32), VM((10 * B, 4 * O * O), BF),
         VM((4 * O * O, 4 * Z), BF), VM((B * B, Z), F32), VM((2, 8, 8, B * B), BF), VM((2, 8, 8, B * B), BF),
         VM((8, B, R), F32), VM((N, B, R), BF), VM((2, 8, B, R), BF), VM((8, B, R), BF),
         *(VM((N, n, 8 * B), t) for t in (BF, BF, F32) for n in pieces),
         *(VM((8, N, n * B), BF) for _ in range(2) for n in pieces),
         pltpu.SemaphoreType.DMA((S,)), pltpu.SemaphoreType.DMA((S,)), pltpu.SemaphoreType.DMA((9,)),
         pltpu.SemaphoreType.DMA((17,))],
        pltpu.HBM,
    )


def solution(mesh):
    tile = PartitionSpec("row", "col", None)
    return jax.shard_map(
        shards,
        mesh=mesh,
        in_specs=(tile, tile) + (PartitionSpec(),) * 7,
        out_specs=(tile, tile),
        check_vma=False,
    )
```

```python
import functools

import jax
import jax.numpy as jnp
from jax import lax
from jax.experimental import pallas as pl
from jax.experimental.pallas import tpu as pltpu
from jax.sharding import PartitionSpec

MESH = pl.DeviceIdType.MESH
EPS = 1e-05
N = 16
AROUND = (1, 7, 2, 6, 3, 5, 4, 0)
AROUND_16 = (1, 15, 2, 14, 3, 13, 4, 12, 5, 11, 6, 10, 7, 9, 8)
BF = jnp.bfloat16
F32 = jnp.float32


def standardize(v, axis=-1):
    v = v.astype(F32)
    center = v - jnp.mean(v, axis=axis, keepdims=True)
    spread = jnp.mean(center * center, axis=axis, keepdims=True)
    return center * lax.rsqrt(spread + EPS)


def here():
    return lax.axis_index("row"), lax.axis_index("col")


def push(src, dst, send, recv, to):
    pltpu.make_async_remote_copy(src, dst, send, recv, device_id=to, device_id_type=MESH).start()


def local(src, dst, recv):
    pltpu.make_async_copy(src, dst, recv).start()


def drain(ref, sem):
    pltpu.make_async_copy(ref, ref, sem).wait()


def greet(to):
    pl.semaphore_signal(pltpu.get_barrier_semaphore(), inc=1, device_id=to, device_id_type=MESH)


def greeted(count):
    pl.semaphore_wait(pltpu.get_barrier_semaphore(), count)


def comm_call(body, name, collective_id, outs, ins, sems, scratch=(), place=pltpu.VMEM):
    return pl.pallas_call(
        body,
        name=name,
        out_shape=outs,
        in_specs=[pl.BlockSpec(memory_space=place)] * len(ins),
        out_specs=[pl.BlockSpec(memory_space=place)] * len(outs),
        scratch_shapes=[*scratch, pltpu.SemaphoreType.DMA((sems,))],
        compiler_params=pltpu.CompilerParams(
            collective_id=collective_id, has_side_effects=True, vmem_limit_bytes=62 << 20
        ),
    )(*ins)


def block_body(
    x_in, pair_in, w_in_in, w_out_in, w_bias_in, w_sides_in, w_outer_in, w_tri_in, w_last_in,
    x_out, pair_out,
    x, pair, w_in, w_out, w_bias, w_sides, w_outer, w_tri, w_last,
    x_new, got, mid, gate, pair_new, xs, bias_out, bias_in, biases, bias, q_all, gates, v_all, scores_all, gated,
    flat, left, right, chunk, lefts, rights, left_s, right_s, tall, stacked, w_wide, normed,
    left_edge, right_edge, spreads, parts, held, mates, sums_0, sums_1, channel_0, channel_1, back_0, back_1,
    outgoing_0, outgoing_1, tiles_0, tiles_1,
    near, far, aside, across, load, back_sem, sem,
):
    sums, channel, back = (sums_0, sums_1), (channel_0, channel_1), (back_0, back_1)
    outgoing, tiles = (outgoing_0, outgoing_1), (tiles_0, tiles_1)
    r, c = here()
    core = lax.rem(c, 2)
    mate = c + 1 - 2 * core
    mine = c // 2
    beside = mine + 1 - 2 * lax.rem(mine, 2)
    opposite = lax.rem(mine + 4, 8)
    ahead, behind = lax.rem(c + 4, N), lax.rem(c + 12, N)
    parity = lax.rem(r, 2)
    S, B, C = x.shape
    H = w_bias.shape[0]
    D = C // H
    O = w_sides.shape[0] // 2
    Z = pair.shape[2]
    G = B // 4
    P = bias_out.shape[0]
    loads = [
        pltpu.make_async_copy(src, dst, load.at[k])
        for k, (src, dst) in enumerate(
            (
                (pair_in, pair), (w_bias_in, w_bias), (x_in, x), (w_in_in, w_in), (w_out_in, w_out),
                (w_sides_in, w_sides), (w_outer_in, w_outer), (w_tri_in, w_tri),
                (w_last_in, w_last),
            )
        )
    ]
    for cp in loads:
        cp.start()
    for s in range(1, N):
        greet((r, lax.rem(c + s, N)))
    for s in range(1, N):
        greet((lax.rem(r + s, N), c))

    @pl.when(r < P)
    def _():
        for s in range(N):
            k = lax.rem(c + s, N)

            @pl.when((c != r) | (k != c))
            def _():
                greet((c, k))

    for s in range(8):
        k = 2 * lax.rem(mine + s, 8) + core

        @pl.when((k != r) | (r != c))
        def _():
            greet((k, r))

    loads[0].wait()
    loads[1].wait()
    pair_n = standardize(pair[...]).astype(BF).reshape(B * B, Z)
    bias_flat = lax.dot_general(
        w_bias[...], pair_n, (((1,), (1,)), ((), ())), preferred_element_type=F32
    )
    bias_flat = jnp.concatenate([bias_flat, jnp.zeros((H, P * 128 - B * B), F32)], 1).astype(BF)
    for k in range(P):
        bias_out[k] = bias_flat[:, k * 128 : (k + 1) * 128]
    own_p = (r == c) & (r < P)
    greeted(38 + P - jnp.where(r == c, 1, 0) - jnp.where(own_p, 1, 0))
    for s in range(P):
        k = lax.rem(s + c, P)
        own = (k == r) & (r == c)

        @pl.when(jnp.logical_not(own))
        def _():
            push(bias_out.at[k], bias_in.at[c], sem.at[10], sem.at[11], (k, r))

        @pl.when(own)
        def _():
            local(bias_out.at[k], bias_in.at[c], sem.at[11])

    @pl.loop(0, S)
    def _(s):
        block = xs.at[s, core, mine]
        push(x_in.at[s], block, sem.at[12], aside.at[s], (r, 2 * beside + core))
        push(x_in.at[s], block, sem.at[12], across.at[s], (r, 2 * opposite + core))
        for to in (ahead, behind):
            push(x_in.at[s], block, sem.at[12], near.at[s], (r, to))
        local(x_in.at[s], xs.at[s, core, mine], near.at[s])

    @pl.when(r < P)
    def _():
        drain(bias_in, sem.at[11])
        for s in AROUND_16:
            push(bias_in, biases.at[r], sem.at[4], sem.at[5], (lax.rem(r + s, N), c))
        local(bias_in, biases.at[r], sem.at[5])

    def relay(s):
        block = xs.at[s, core, beside]
        drain(block, aside.at[s])
        for to in (ahead, behind):
            push(block, block, sem.at[12], near.at[s], (r, to))
        block = xs.at[s, core, opposite]
        drain(block, across.at[s])
        push(block, block, sem.at[12], near.at[s], (r, 2 * beside + core))

    def forward(s):
        drain(xs.at[s, core, pl.ds(0, 6)], near.at[s])
        push(xs.at[s, core], xs.at[s, core], sem.at[13], far.at[s], (r, mate))

    for cp in loads[2:]:
        cp.wait()
    own_n = standardize(x[...]).astype(BF).reshape(S * B, C)
    q = jnp.dot(own_n, w_in[:, :C], preferred_element_type=F32) * D ** (-0.5)
    q_all[...] = q.reshape(S, B, C)
    gates[...] = jax.nn.sigmoid(jnp.dot(own_n, w_in[:, 3 * C :], preferred_element_type=F32))
    w_wide[...] = jnp.zeros_like(w_wide)
    tall[pl.ds(0, O * O), :] = w_outer[...].astype(F32)
    for d in range(O):
        part = tall[pl.ds(d, O, stride=O), :].astype(BF)
        for i in range(4):
            w_wide[pl.ds(d * 4 * O + i * O, O), i * Z : (i + 1) * Z] = part
    head = lax.broadcasted_iota(jnp.int32, (B, C), 1) // D
    relay(0)
    relay(1)
    forward(0)

    @pl.loop(0, S)
    def _(s):
        @pl.when(s < S - 2)
        def _():
            relay(s + 2)

        @pl.when(s < S - 1)
        def _():
            forward(s + 1)

        drain(xs.at[s, 1 - core], far.at[s])
        x_s = standardize(xs[s]).reshape(N * B, C).astype(BF)
        k = jnp.dot(x_s, w_in[:, C : 2 * C], preferred_element_type=F32).astype(BF)
        v_all[s] = jnp.dot(x_s, w_in[:, 2 * C : 3 * C], preferred_element_type=F32).astype(BF)
        q_s = q_all[s]
        q_h = jnp.concatenate([jnp.where(head == h, q_s, 0.0) for h in range(H)], 0).astype(BF)
        scores_all[s] = lax.dot_general(
            q_h, k, (((1,), (1,)), ((), ())), preferred_element_type=F32
        )

    drain(bias_out.at[pl.ds(0, P - 1)], sem.at[10])

    @pl.when(jnp.logical_not(own_p))
    def _():
        drain(bias_out.at[0], sem.at[10])

    @pl.when(r < P)
    def _():
        for s in range(1, N):
            drain(bias_in, sem.at[4])

    drain(biases, sem.at[5])

    def bias_of(k):
        block = 2 * (k % 8) + k // 8
        return jnp.concatenate([biases[p, block].astype(F32) for p in range(P)], 1)

    spread(bias_of, bias, B)
    for half in range(2):
        first, count = half * S // 2, S // 2

        @pl.loop(first, first + count)
        def _(s):
            scores = scores_all[s] + bias[...].reshape(H * B, N * B)
            e = jnp.exp(scores - jnp.max(scores, -1, keepdims=True))
            att = jnp.dot(e.astype(BF), v_all[s], preferred_element_type=F32)
            att = (att / jnp.sum(e, -1, keepdims=True)).reshape(H, B, C)
            total = jnp.where(head == 0, att[0], 0.0)
            for h in range(1, H):
                total = jnp.where(head == h, att[h], total)
            gated[pl.ds(pl.multiple_of(s * B, 8), B), :] = total

        span = slice(first * B, (first + count) * B)
        update = jnp.dot(
            (gated[span] * gates[span]).astype(BF), w_out[...], preferred_element_type=F32
        )
        x_half = (
            x[first : first + count].astype(F32) + update.reshape(count, B, C)
        ).astype(BF)
        x_new[first : first + count] = x_half
        flat[span, : 2 * O] = lax.dot_general(
            standardize(x_half).astype(BF).reshape(count * B, C), w_sides[...],
            (((1,), (1,)), ((), ())), preferred_element_type=F32,
        )
        for k, side in ((0, left), (O, right)):
            lanes = jnp.concatenate(
                [flat[pl.ds(first * B + u, count * G, stride=4), :][:, k : k + O] for u in range(4)], 1
            )
            for s in range(count):
                side[first + s] = lanes[s * G : (s + 1) * G].astype(BF)
        for s in range(first, first + count):
            k = 2 * s + parity
            own = (k == c) & (r == c)

            @pl.when(jnp.logical_not(own))
            def _():
                push(left.at[s], chunk.at[r // 2], sem.at[0], sem.at[1], (c, k))

            @pl.when(own)
            def _():
                local(left.at[s], chunk.at[r // 2], sem.at[1])

        part = right.at[pl.ds(first, count)]
        there = rights.at[parity, pl.ds(first, count), r // 2]
        for s in AROUND_16:
            push(part, there, sem.at[2], sem.at[3], (lax.rem(r + s, N), c))
        local(part, there, sem.at[3])
    x_done = pltpu.make_async_copy(x_new, x_out, load.at[0])
    x_done.start()
    drain(chunk, sem.at[1])
    for s in AROUND[:-1]:
        push(chunk, lefts.at[core, mine], sem.at[6], sem.at[7], (r, lax.rem(c + 2 * s, N)))
    local(chunk, lefts.at[core, mine], sem.at[7])
    for g in range(7):
        drain(xs.at[:, 0, 0], sem.at[12])
    drain(xs.at[:, 0], sem.at[13])
    drain(lefts.at[core], sem.at[7])
    push(lefts.at[core], lefts.at[core], sem.at[8], sem.at[9], (r, mate))
    drain(chunk.at[pl.ds(0, 7)], sem.at[0])

    @pl.when(r != c)
    def _():
        drain(chunk.at[0], sem.at[0])

    for s in range(N - 1):
        drain(right, sem.at[2])
    drain(lefts.at[0, pl.ds(0, 7)], sem.at[6])
    drain(rights, sem.at[3])
    right_s[...] = rights[...].astype(F32).reshape(S * N, G, 4 * O)
    for k in range(G):
        tall[pl.ds(k * 4 * O, 4 * O), :] = right_s[:, k, :].T
    right_t = jnp.concatenate([tall[pl.ds(d, B, stride=O), :] for d in range(O)], 0).astype(BF)
    drain(lefts.at[0], sem.at[8])
    drain(lefts.at[1 - core], sem.at[9])
    left_s[...] = lefts[...].astype(F32).reshape(S * N, G, 4 * O)
    for g in range(B // 8):
        halves = [
            jnp.dot(right_t, left_s[:, k, :].astype(BF), preferred_element_type=F32)
            * (1.0 / (S * N))
            for k in (2 * g, 2 * g + 1)
        ]
        for d in range(O):
            stacked[pl.ds(g * 2 * B, 2 * B), d * 4 * O : (d + 1) * 4 * O] = jnp.concatenate(
                [h[d * B : (d + 1) * B] for h in halves], 0
            ).astype(BF)
    wide = jnp.dot(stacked[...], w_wide[...], preferred_element_type=F32)
    for i in range(B):
        k, u = i // 4, i % 4
        row = (pair[i].astype(F32) + wide[k * B : (k + 1) * B, u * Z : (u + 1) * Z]).astype(BF)
        mid[i] = row
        normed[pl.ds(i * B, B), :] = standardize(row)
    tri_n = normed[...].astype(BF)

    def edge(k):
        w = w_tri[:, 2 * k * Z : 2 * (k + 1) * Z]
        both = lax.dot_general(w, tri_n, (((0,), (1,)), ((), ())), preferred_element_type=F32)
        return (jax.nn.sigmoid(both[Z:]) * both[:Z]).reshape(8, 2, 8, B * B)

    def over_col(k, h):
        ref = (left_edge, right_edge)[k]
        for s in AROUND:
            g = lax.rem(mine + s, 8)
            to = 2 * g + lax.rem(parity + 1 + k, 2)
            if s == 0:

                @pl.when(to != c)
                def _():
                    push(ref.at[h, g], got.at[h, c], back_sem.at[14], back_sem.at[15 + h], (r, to))

                @pl.when(to == c)
                def _():
                    local(ref.at[h, g], got.at[h, c], back_sem.at[15 + h])
            else:
                push(ref.at[h, g], got.at[h, c], back_sem.at[14], back_sem.at[15 + h], (r, to))

    for k, ref in ((0, left_edge), (1, right_edge)):
        values = edge(k)
        for h in range(2):
            ref[h] = values[:, h].astype(BF)
        over_col(k, 0)
    over_col(0, 1)
    over_col(1, 1)
    gate[...] = jax.nn.sigmoid(jnp.dot(tri_n, w_tri[:, 4 * Z :], preferred_element_type=F32))
    kind = lax.rem(r + core, 2)
    R = N * B
    arrived = back_sem.at[1 + 2 * parity + r // 8]
    for h in range(2):
        drain(got.at[h], back_sem.at[15 + h])
        spread(lambda k: got[h, k].astype(F32), spreads, B)
        parts[pl.ds(8 * h, 8)] = spreads[...].astype(BF)
        for s in AROUND:
            q = 8 * h + lax.rem(r + s, 8)
            if s == 0:

                @pl.when(q != r)
                def _():
                    push(parts.at[q], held.at[kind, r // 2], back_sem.at[0], arrived, (q, c))

                @pl.when(q == r)
                def _():
                    local(parts.at[q], held.at[kind, r // 2], arrived)
            else:
                push(parts.at[q], held.at[kind, r // 2], back_sem.at[0], arrived, (q, c))
    for h in range(2):
        some = held.at[1, pl.ds(4 * h, 4)]
        drain(some, back_sem.at[3 - 2 * core + h])
        push(some, mates.at[pl.ds(4 * h, 4)], back_sem.at[5], back_sem.at[6], (r, mate))
    for h in range(2):
        drain(held.at[0, pl.ds(4 * h, 4)], back_sem.at[1 + 2 * core + h])
    columns = held[0].reshape(8 * B, R)
    rows = ((0, B * 3 // 5), (B * 3 // 5, B))

    def products(ref):
        return lax.dot_general(
            ref.reshape(8 * B, R), columns, (((1,), (1,)), ((), ())), preferred_element_type=F32
        )

    def over_row(piece, odd):
        for s in AROUND:
            q = 2 * lax.rem(r // 2 + s, 8) + odd

            @pl.when(q != r)
            def _():
                push(sums[piece].at[q], channel[piece].at[r], back_sem.at[7], back_sem.at[8 + piece], (q, c))

            @pl.when(q == r)
            def _():
                local(sums[piece].at[q], channel[piece].at[r], back_sem.at[8 + piece])

    for ref, odd in ((held.at[1], 1 - core), (mates, core)):
        if ref is mates:
            drain(mates, back_sem.at[6])
        total = products(ref[...])
        for piece, (low, high) in enumerate(rows):
            for s in range(8):
                sums[piece][2 * s + odd] = total[s * B + low : s * B + high].astype(BF)
            if piece == 0:
                over_row(0, odd)
    over_row(1, 1 - core)
    over_row(1, core)
    drain(parts.at[pl.ds(0, N - 1)], back_sem.at[0])
    drain(mates, back_sem.at[5])
    for piece in range(2):
        drain(channel[piece], back_sem.at[8 + piece])
        back[piece][...] = channel[piece][...].astype(F32)
        lines = [back[piece][:, i, :] for i in range(back[piece].shape[1])]
        for g in range(8):
            outgoing[piece][g] = jnp.concatenate([v[:, g * B : (g + 1) * B] for v in lines], 1).astype(BF)
        for s in AROUND[:-1]:
            g = lax.rem(mine + s, 8)
            push(
                outgoing[piece].at[g], tiles[piece].at[mine], back_sem.at[10], back_sem.at[11 + piece],
                (r, 2 * g + core),
            )
        local(outgoing[piece].at[mine], tiles[piece].at[mine], back_sem.at[11 + piece])
    for piece, (low, high) in enumerate(rows):
        drain(tiles[piece], back_sem.at[11 + piece])
        tri_ln = standardize(tiles[piece][...].reshape(Z, (high - low) * B), 0).astype(BF)
        update = lax.dot_general(
            tri_ln, w_last[...], (((0,), (0,)), ((), ())), preferred_element_type=F32
        )
        pair_new[low:high] = (
            mid[low:high].astype(F32)
            + (gate[low * B : high * B, :] * update).reshape(high - low, B, Z)
        ).astype(BF)
    for piece in range(2):
        drain(sums[piece].at[pl.ds(0, N - 1)], back_sem.at[7])
        drain(outgoing[piece].at[pl.ds(0, 7)], back_sem.at[10])
    for h in range(2):
        drain(got.at[h, pl.ds(0, N - 1)], back_sem.at[14])
    done = pltpu.make_async_copy(pair_new, pair_out, back_sem.at[13])
    done.start()
    done.wait()
    x_done.wait()


def spread(block, out, B):
    blocks = [block(k) for k in range(N)]
    for i in range(B):
        out[:, i, :] = jnp.concatenate([b[:, i * B : (i + 1) * B] for b in blocks], 1)


def like(shape, dtype=BF):
    return jax.ShapeDtypeStruct(shape, dtype)


def shards(x, pair, w_in, w_out, w_bias, w_sides, w_outer, w_tri, w_tri_out):
    core = lax.rem(lax.axis_index("col"), 2)
    S, B, C = x.shape
    Z = pair.shape[2]
    H = w_bias.shape[1]
    O = w_sides.shape[1] // 2
    G = B // 4
    SP = S * N
    R = B * N
    P = -(-B * B // 128)
    pieces = (B * 3 // 5, B - B * 3 // 5)

    VM = pltpu.VMEM
    args = [x, pair, w_in, w_out, w_bias.T, w_sides.T, w_outer, w_tri, w_tri_out]
    return comm_call(
        block_body, "block", 1, [like((S, B, C)), like((B, B, Z))], args, 16,
        [*(VM(v.shape, BF) for v in args),
         VM((S, B, C), BF), VM((2, N, 8, B * B), BF), VM((B, B, Z), BF), VM((B * B, Z), F32), VM((B, B, Z), BF),
         VM((S, 2, 8, B, C), BF), VM((P, H, 128), BF), VM((N, H, 128), BF), VM((P, N, H, 128), BF), VM((H, B, R), F32),
         VM((S, B, C), F32), VM((S * B, C), F32), VM((S, R, C), BF), VM((S, H * B, R), F32),
         VM((S * B, C), F32),
         VM((S * B, 128), F32), VM((S, G, 4 * O), BF), VM((S, G, 4 * O), BF), VM((8, G, 4 * O), BF),
         VM((2, S, 8, G, 4 * O), BF), VM((2, S, 8, G, 4 * O), BF), VM((SP, G, 4 * O), F32),
         VM((SP, G, 4 * O), F32), VM((B * O, SP), F32), VM((10 * B, 4 * O * O), BF),
         VM((4 * O * O, 4 * Z), BF), VM((B * B, Z), F32), VM((2, 8, 8, B * B), BF), VM((2, 8, 8, B * B), BF),
         VM((8, B, R), F32), VM((N, B, R), BF), VM((2, 8, B, R), BF), VM((8, B, R), BF),
         *(VM((N, n, 8 * B), t) for t in (BF, BF, F32) for n in pieces),
         *(VM((8, N, n * B), BF) for _ in range(2) for n in pieces),
         *(pltpu.SemaphoreType.DMA((S,)) for _ in range(4)), pltpu.SemaphoreType.DMA((9,)),
         pltpu.SemaphoreType.DMA((17,))],
        pltpu.HBM,
    )


def solution(mesh):
    tile = PartitionSpec("row", "col", None)
    return jax.shard_map(
        shards,
        mesh=mesh,
        in_specs=(tile, tile) + (PartitionSpec(),) * 7,
        out_specs=(tile, tile),
        check_vma=False,
    )
```

```python
import functools

import jax
import jax.numpy as jnp
from jax import lax
from jax.experimental import pallas as pl
from jax.experimental.pallas import tpu as pltpu
from jax.sharding import PartitionSpec

MESH = pl.DeviceIdType.MESH
EPS = 1e-05
N = 16
AROUND = (1, 7, 2, 6, 3, 5, 4, 0)
AROUND_16 = (1, 15, 2, 14, 3, 13, 4, 12, 5, 11, 6, 10, 7, 9, 8)
BF = jnp.bfloat16
F32 = jnp.float32


def standardize(v, axis=-1):
    v = v.astype(F32)
    center = v - jnp.mean(v, axis=axis, keepdims=True)
    spread = jnp.mean(center * center, axis=axis, keepdims=True)
    return center * lax.rsqrt(spread + EPS)


def here():
    return lax.axis_index("row"), lax.axis_index("col")


def push(src, dst, send, recv, to):
    pltpu.make_async_remote_copy(src, dst, send, recv, device_id=to, device_id_type=MESH).start()


def local(src, dst, recv):
    pltpu.make_async_copy(src, dst, recv).start()


def drain(ref, sem):
    pltpu.make_async_copy(ref, ref, sem).wait()


def greet(to):
    pl.semaphore_signal(pltpu.get_barrier_semaphore(), inc=1, device_id=to, device_id_type=MESH)


def greeted(count):
    pl.semaphore_wait(pltpu.get_barrier_semaphore(), count)


def comm_call(body, name, collective_id, outs, ins, sems, scratch=(), place=pltpu.VMEM):
    return pl.pallas_call(
        body,
        name=name,
        out_shape=outs,
        in_specs=[pl.BlockSpec(memory_space=place)] * len(ins),
        out_specs=[pl.BlockSpec(memory_space=place)] * len(outs),
        scratch_shapes=[*scratch, pltpu.SemaphoreType.DMA((sems,))],
        compiler_params=pltpu.CompilerParams(
            collective_id=collective_id, has_side_effects=True, vmem_limit_bytes=62 << 20
        ),
    )(*ins)


def block_body(
    x_in, pair_in, w_in_in, w_out_in, w_bias_in, w_sides_in, w_outer_in, w_tri_in, w_last_in,
    x_out, pair_out,
    x, pair, w_in, w_out, w_bias, w_sides, w_outer, w_tri, w_last,
    x_new, got, mid, gate, pair_new, xs, bias_out, bias_in, biases, bias, q_all, gates, v_all, scores_all, gated,
    flat, left, right, chunk, lefts, rights, left_s, right_s, tall, stacked, w_wide, normed,
    left_edge, right_edge, spreads, parts, held, mates, sums_0, sums_1, channel_0, channel_1, back_0, back_1,
    outgoing_0, outgoing_1, tiles_0, tiles_1,
    near, far, load, back_sem, sem,
):
    sums, channel, back = (sums_0, sums_1), (channel_0, channel_1), (back_0, back_1)
    outgoing, tiles = (outgoing_0, outgoing_1), (tiles_0, tiles_1)
    r, c = here()
    core = lax.rem(c, 2)
    mate = c + 1 - 2 * core
    mine = c // 2
    parity = lax.rem(r, 2)
    S, B, C = x.shape
    H = w_bias.shape[0]
    D = C // H
    O = w_sides.shape[0] // 2
    Z = pair.shape[2]
    G = B // 4
    P = bias_out.shape[0]
    loads = [
        pltpu.make_async_copy(src, dst, load.at[k])
        for k, (src, dst) in enumerate(
            (
                (pair_in, pair), (w_bias_in, w_bias), (x_in, x), (w_in_in, w_in), (w_out_in, w_out),
                (w_sides_in, w_sides), (w_outer_in, w_outer), (w_tri_in, w_tri),
                (w_last_in, w_last),
            )
        )
    ]
    for cp in loads:
        cp.start()
    for s in range(1, N):
        greet((r, lax.rem(c + s, N)))
    for s in range(1, N):
        greet((lax.rem(r + s, N), c))

    @pl.when(r < P)
    def _():
        for s in range(N):
            k = lax.rem(c + s, N)

            @pl.when((c != r) | (k != c))
            def _():
                greet((c, k))

    for s in range(8):
        k = 2 * lax.rem(mine + s, 8) + core

        @pl.when((k != r) | (r != c))
        def _():
            greet((k, r))

    loads[0].wait()
    loads[1].wait()
    pair_n = standardize(pair[...]).astype(BF).reshape(B * B, Z)
    bias_flat = lax.dot_general(
        w_bias[...], pair_n, (((1,), (1,)), ((), ())), preferred_element_type=F32
    )
    bias_flat = jnp.concatenate([bias_flat, jnp.zeros((H, P * 128 - B * B), F32)], 1).astype(BF)
    for k in range(P):
        bias_out[k] = bias_flat[:, k * 128 : (k + 1) * 128]
    own_p = (r == c) & (r < P)
    greeted(38 + P - jnp.where(r == c, 1, 0) - jnp.where(own_p, 1, 0))
    for s in range(P):
        k = lax.rem(s + c, P)
        own = (k == r) & (r == c)

        @pl.when(jnp.logical_not(own))
        def _():
            push(bias_out.at[k], bias_in.at[c], sem.at[10], sem.at[11], (k, r))

        @pl.when(own)
        def _():
            local(bias_out.at[k], bias_in.at[c], sem.at[11])

    @pl.loop(0, S)
    def _(s):
        for g in AROUND[:-1]:
            push(x_in.at[s], xs.at[s, core, mine], sem.at[12], near.at[s], (r, lax.rem(c + 2 * g, N)))
        local(x_in.at[s], xs.at[s, core, mine], near.at[s])

    @pl.when(r < P)
    def _():
        drain(bias_in, sem.at[11])
        for s in AROUND_16:
            push(bias_in, biases.at[r], sem.at[4], sem.at[5], (lax.rem(r + s, N), c))
        local(bias_in, biases.at[r], sem.at[5])

    def forward(s):
        drain(xs.at[s, core], near.at[s])
        push(xs.at[s, core], xs.at[s, core], sem.at[13], far.at[s], (r, mate))

    for cp in loads[2:]:
        cp.wait()
    own_n = standardize(x[...]).astype(BF).reshape(S * B, C)
    q = jnp.dot(own_n, w_in[:, :C], preferred_element_type=F32) * D ** (-0.5)
    q_all[...] = q.reshape(S, B, C)
    gates[...] = jax.nn.sigmoid(jnp.dot(own_n, w_in[:, 3 * C :], preferred_element_type=F32))
    w_wide[...] = jnp.zeros_like(w_wide)
    tall[pl.ds(0, O * O), :] = w_outer[...].astype(F32)
    for d in range(O):
        part = tall[pl.ds(d, O, stride=O), :].astype(BF)
        for i in range(4):
            w_wide[pl.ds(d * 4 * O + i * O, O), i * Z : (i + 1) * Z] = part
    head = lax.broadcasted_iota(jnp.int32, (B, C), 1) // D
    forward(0)

    @pl.loop(0, S)
    def _(s):
        @pl.when(s < S - 1)
        def _():
            forward(s + 1)

        drain(xs.at[s, 1 - core], far.at[s])
        x_s = standardize(xs[s]).reshape(N * B, C).astype(BF)
        k = jnp.dot(x_s, w_in[:, C : 2 * C], preferred_element_type=F32).astype(BF)
        v_all[s] = jnp.dot(x_s, w_in[:, 2 * C : 3 * C], preferred_element_type=F32).astype(BF)
        q_s = q_all[s]
        q_h = jnp.concatenate([jnp.where(head == h, q_s, 0.0) for h in range(H)], 0).astype(BF)
        scores_all[s] = lax.dot_general(
            q_h, k, (((1,), (1,)), ((), ())), preferred_element_type=F32
        )

    drain(bias_out.at[pl.ds(0, P - 1)], sem.at[10])

    @pl.when(jnp.logical_not(own_p))
    def _():
        drain(bias_out.at[0], sem.at[10])

    @pl.when(r < P)
    def _():
        for s in range(1, N):
            drain(bias_in, sem.at[4])

    drain(biases, sem.at[5])

    def bias_of(k):
        block = 2 * (k % 8) + k // 8
        return jnp.concatenate([biases[p, block].astype(F32) for p in range(P)], 1)

    spread(bias_of, bias, B)
    for half in range(2):
        first, count = half * S // 2, S // 2

        @pl.loop(first, first + count, unroll=2)
        def _(s):
            scores = scores_all[s] + bias[...].reshape(H * B, N * B)
            e = jnp.exp(scores - jnp.max(scores, -1, keepdims=True))
            att = jnp.dot(e.astype(BF), v_all[s], preferred_element_type=F32)
            att = (att / jnp.sum(e, -1, keepdims=True)).reshape(H, B, C)
            total = jnp.where(head == 0, att[0], 0.0)
            for h in range(1, H):
                total = jnp.where(head == h, att[h], total)
            gated[pl.ds(pl.multiple_of(s * B, 8), B), :] = total

        span = slice(first * B, (first + count) * B)
        update = jnp.dot(
            (gated[span] * gates[span]).astype(BF), w_out[...], preferred_element_type=F32
        )
        x_half = (
            x[first : first + count].astype(F32) + update.reshape(count, B, C)
        ).astype(BF)
        x_new[first : first + count] = x_half
        flat[span, : 2 * O] = lax.dot_general(
            standardize(x_half).astype(BF).reshape(count * B, C), w_sides[...],
            (((1,), (1,)), ((), ())), preferred_element_type=F32,
        )
        for k, side in ((0, left), (O, right)):
            lanes = jnp.concatenate(
                [flat[pl.ds(first * B + u, count * G, stride=4), :][:, k : k + O] for u in range(4)], 1
            )
            for s in range(count):
                side[first + s] = lanes[s * G : (s + 1) * G].astype(BF)
        for s in range(first, first + count):
            k = 2 * s + parity
            own = (k == c) & (r == c)

            @pl.when(jnp.logical_not(own))
            def _():
                push(left.at[s], chunk.at[r // 2], sem.at[0], sem.at[1], (c, k))

            @pl.when(own)
            def _():
                local(left.at[s], chunk.at[r // 2], sem.at[1])

        part = right.at[pl.ds(first, count)]
        there = rights.at[parity, pl.ds(first, count), r // 2]
        for s in AROUND_16:
            push(part, there, sem.at[2], sem.at[3], (lax.rem(r + s, N), c))
        local(part, there, sem.at[3])
    x_done = pltpu.make_async_copy(x_new, x_out, load.at[0])
    x_done.start()
    drain(chunk, sem.at[1])
    for s in AROUND[:-1]:
        push(chunk, lefts.at[core, mine], sem.at[6], sem.at[7], (r, lax.rem(c + 2 * s, N)))
    local(chunk, lefts.at[core, mine], sem.at[7])
    for g in range(7):
        drain(xs.at[:, 0, 0], sem.at[12])
    drain(xs.at[:, 0], sem.at[13])
    drain(lefts.at[core], sem.at[7])
    push(lefts.at[core], lefts.at[core], sem.at[8], sem.at[9], (r, mate))
    drain(chunk.at[pl.ds(0, 7)], sem.at[0])

    @pl.when(r != c)
    def _():
        drain(chunk.at[0], sem.at[0])

    for s in range(N - 1):
        drain(right, sem.at[2])
    drain(lefts.at[0, pl.ds(0, 7)], sem.at[6])
    drain(rights, sem.at[3])
    right_s[...] = rights[...].astype(F32).reshape(S * N, G, 4 * O)
    for k in range(G):
        tall[pl.ds(k * 4 * O, 4 * O), :] = right_s[:, k, :].T
    right_t = jnp.concatenate([tall[pl.ds(d, B, stride=O), :] for d in range(O)], 0).astype(BF)
    drain(lefts.at[0], sem.at[8])
    drain(lefts.at[1 - core], sem.at[9])
    left_s[...] = lefts[...].astype(F32).reshape(S * N, G, 4 * O)
    for g in range(B // 8):
        halves = [
            jnp.dot(right_t, left_s[:, k, :].astype(BF), preferred_element_type=F32)
            * (1.0 / (S * N))
            for k in (2 * g, 2 * g + 1)
        ]
        for d in range(O):
            stacked[pl.ds(g * 2 * B, 2 * B), d * 4 * O : (d + 1) * 4 * O] = jnp.concatenate(
                [h[d * B : (d + 1) * B] for h in halves], 0
            ).astype(BF)
    wide = jnp.dot(stacked[...], w_wide[...], preferred_element_type=F32)
    for i in range(B):
        k, u = i // 4, i % 4
        row = (pair[i].astype(F32) + wide[k * B : (k + 1) * B, u * Z : (u + 1) * Z]).astype(BF)
        mid[i] = row
        normed[pl.ds(i * B, B), :] = standardize(row)
    tri_n = normed[...].astype(BF)

    def edge(k):
        w = w_tri[:, 2 * k * Z : 2 * (k + 1) * Z]
        both = lax.dot_general(w, tri_n, (((0,), (1,)), ((), ())), preferred_element_type=F32)
        return (jax.nn.sigmoid(both[Z:]) * both[:Z]).reshape(8, 2, 8, B * B)

    def over_col(k, h):
        ref = (left_edge, right_edge)[k]
        for s in AROUND:
            g = lax.rem(mine + s, 8)
            to = 2 * g + lax.rem(parity + 1 + k, 2)
            if s == 0:

                @pl.when(to != c)
                def _():
                    push(ref.at[h, g], got.at[h, c], back_sem.at[14], back_sem.at[15 + h], (r, to))

                @pl.when(to == c)
                def _():
                    local(ref.at[h, g], got.at[h, c], back_sem.at[15 + h])
            else:
                push(ref.at[h, g], got.at[h, c], back_sem.at[14], back_sem.at[15 + h], (r, to))

    for k, ref in ((0, left_edge), (1, right_edge)):
        values = edge(k)
        for h in range(2):
            ref[h] = values[:, h].astype(BF)
        over_col(k, 0)
    over_col(0, 1)
    over_col(1, 1)
    gate[...] = jax.nn.sigmoid(jnp.dot(tri_n, w_tri[:, 4 * Z :], preferred_element_type=F32))
    kind = lax.rem(r + core, 2)
    R = N * B
    arrived = back_sem.at[1 + 2 * parity + r // 8]
    for h in range(2):
        drain(got.at[h], back_sem.at[15 + h])
        spread(lambda k: got[h, k].astype(F32), spreads, B)
        parts[pl.ds(8 * h, 8)] = spreads[...].astype(BF)
        for s in AROUND:
            q = 8 * h + lax.rem(r + s, 8)
            if s == 0:

                @pl.when(q != r)
                def _():
                    push(parts.at[q], held.at[kind, r // 2], back_sem.at[0], arrived, (q, c))

                @pl.when(q == r)
                def _():
                    local(parts.at[q], held.at[kind, r // 2], arrived)
            else:
                push(parts.at[q], held.at[kind, r // 2], back_sem.at[0], arrived, (q, c))
    for h in range(2):
        some = held.at[1, pl.ds(4 * h, 4)]
        drain(some, back_sem.at[3 - 2 * core + h])
        push(some, mates.at[pl.ds(4 * h, 4)], back_sem.at[5], back_sem.at[6], (r, mate))
    for h in range(2):
        drain(held.at[0, pl.ds(4 * h, 4)], back_sem.at[1 + 2 * core + h])
    columns = held[0].reshape(8 * B, R)
    rows = ((0, B * 3 // 5), (B * 3 // 5, B))

    def products(ref):
        return lax.dot_general(
            ref.reshape(8 * B, R), columns, (((1,), (1,)), ((), ())), preferred_element_type=F32
        )

    def over_row(piece, odd):
        for s in AROUND:
            q = 2 * lax.rem(r // 2 + s, 8) + odd

            @pl.when(q != r)
            def _():
                push(sums[piece].at[q], channel[piece].at[r], back_sem.at[7], back_sem.at[8 + piece], (q, c))

            @pl.when(q == r)
            def _():
                local(sums[piece].at[q], channel[piece].at[r], back_sem.at[8 + piece])

    for ref, odd in ((held.at[1], 1 - core), (mates, core)):
        if ref is mates:
            drain(mates, back_sem.at[6])
        total = products(ref[...])
        for piece, (low, high) in enumerate(rows):
            for s in range(8):
                sums[piece][2 * s + odd] = total[s * B + low : s * B + high].astype(BF)
            if piece == 0:
                over_row(0, odd)
    over_row(1, 1 - core)
    over_row(1, core)
    drain(parts.at[pl.ds(0, N - 1)], back_sem.at[0])
    drain(mates, back_sem.at[5])
    for piece in range(2):
        drain(channel[piece], back_sem.at[8 + piece])
        back[piece][...] = channel[piece][...].astype(F32)
        lines = [back[piece][:, i, :] for i in range(back[piece].shape[1])]
        for g in range(8):
            outgoing[piece][g] = jnp.concatenate([v[:, g * B : (g + 1) * B] for v in lines], 1).astype(BF)
        for s in AROUND[:-1]:
            g = lax.rem(mine + s, 8)
            push(
                outgoing[piece].at[g], tiles[piece].at[mine], back_sem.at[10], back_sem.at[11 + piece],
                (r, 2 * g + core),
            )
        local(outgoing[piece].at[mine], tiles[piece].at[mine], back_sem.at[11 + piece])
    for piece, (low, high) in enumerate(rows):
        drain(tiles[piece], back_sem.at[11 + piece])
        tri_ln = standardize(tiles[piece][...].reshape(Z, (high - low) * B), 0).astype(BF)
        update = lax.dot_general(
            tri_ln, w_last[...], (((0,), (0,)), ((), ())), preferred_element_type=F32
        )
        pair_new[low:high] = (
            mid[low:high].astype(F32)
            + (gate[low * B : high * B, :] * update).reshape(high - low, B, Z)
        ).astype(BF)
    for piece in range(2):
        drain(sums[piece].at[pl.ds(0, N - 1)], back_sem.at[7])
        drain(outgoing[piece].at[pl.ds(0, 7)], back_sem.at[10])
    for h in range(2):
        drain(got.at[h, pl.ds(0, N - 1)], back_sem.at[14])
    done = pltpu.make_async_copy(pair_new, pair_out, back_sem.at[13])
    done.start()
    done.wait()
    x_done.wait()


def spread(block, out, B):
    blocks = [block(k) for k in range(N)]
    for i in range(B):
        out[:, i, :] = jnp.concatenate([b[:, i * B : (i + 1) * B] for b in blocks], 1)


def like(shape, dtype=BF):
    return jax.ShapeDtypeStruct(shape, dtype)


def shards(x, pair, w_in, w_out, w_bias, w_sides, w_outer, w_tri, w_tri_out):
    core = lax.rem(lax.axis_index("col"), 2)
    S, B, C = x.shape
    Z = pair.shape[2]
    H = w_bias.shape[1]
    O = w_sides.shape[1] // 2
    G = B // 4
    SP = S * N
    R = B * N
    P = -(-B * B // 128)
    pieces = (B * 3 // 5, B - B * 3 // 5)

    VM = pltpu.VMEM
    args = [x, pair, w_in, w_out, w_bias.T, w_sides.T, w_outer, w_tri, w_tri_out]
    return comm_call(
        block_body, "block", 1, [like((S, B, C)), like((B, B, Z))], args, 16,
        [*(VM(v.shape, BF) for v in args),
         VM((S, B, C), BF), VM((2, N, 8, B * B), BF), VM((B, B, Z), BF), VM((B * B, Z), F32), VM((B, B, Z), BF),
         VM((S, 2, 8, B, C), BF), VM((P, H, 128), BF), VM((N, H, 128), BF), VM((P, N, H, 128), BF), VM((H, B, R), F32),
         VM((S, B, C), F32), VM((S * B, C), F32), VM((S, R, C), BF), VM((S, H * B, R), F32),
         VM((S * B, C), F32),
         VM((S * B, 128), F32), VM((S, G, 4 * O), BF), VM((S, G, 4 * O), BF), VM((8, G, 4 * O), BF),
         VM((2, S, 8, G, 4 * O), BF), VM((2, S, 8, G, 4 * O), BF), VM((SP, G, 4 * O), F32),
         VM((SP, G, 4 * O), F32), VM((B * O, SP), F32), VM((10 * B, 4 * O * O), BF),
         VM((4 * O * O, 4 * Z), BF), VM((B * B, Z), F32), VM((2, 8, 8, B * B), BF), VM((2, 8, 8, B * B), BF),
         VM((8, B, R), F32), VM((N, B, R), BF), VM((2, 8, B, R), BF), VM((8, B, R), BF),
         *(VM((N, n, 8 * B), t) for t in (BF, BF, F32) for n in pieces),
         *(VM((8, N, n * B), BF) for _ in range(2) for n in pieces),
         pltpu.SemaphoreType.DMA((S,)), pltpu.SemaphoreType.DMA((S,)), pltpu.SemaphoreType.DMA((9,)),
         pltpu.SemaphoreType.DMA((17,))],
        pltpu.HBM,
    )


def solution(mesh):
    tile = PartitionSpec("row", "col", None)
    return jax.shard_map(
        shards,
        mesh=mesh,
        in_specs=(tile, tile) + (PartitionSpec(),) * 7,
        out_specs=(tile, tile),
        check_vma=False,
    )
```

```python
import functools

import jax
import jax.numpy as jnp
from jax import lax
from jax.experimental import pallas as pl
from jax.experimental.pallas import tpu as pltpu
from jax.sharding import PartitionSpec

MESH = pl.DeviceIdType.MESH
EPS = 1e-05
N = 16
AROUND = (1, 7, 2, 6, 3, 5, 4, 0)
AROUND_16 = (1, 15, 2, 14, 3, 13, 4, 12, 5, 11, 6, 10, 7, 9, 8)
BF = jnp.bfloat16
F32 = jnp.float32


def standardize(v, axis=-1):
    v = v.astype(F32)
    center = v - jnp.mean(v, axis=axis, keepdims=True)
    spread = jnp.mean(center * center, axis=axis, keepdims=True)
    return center * lax.rsqrt(spread + EPS)


def here():
    return lax.axis_index("row"), lax.axis_index("col")


def push(src, dst, send, recv, to):
    pltpu.make_async_remote_copy(src, dst, send, recv, device_id=to, device_id_type=MESH).start()


def local(src, dst, recv):
    pltpu.make_async_copy(src, dst, recv).start()


def drain(ref, sem):
    pltpu.make_async_copy(ref, ref, sem).wait()


def greet(to):
    pl.semaphore_signal(pltpu.get_barrier_semaphore(), inc=1, device_id=to, device_id_type=MESH)


def greeted(count):
    pl.semaphore_wait(pltpu.get_barrier_semaphore(), count)


def comm_call(body, name, collective_id, outs, ins, sems, scratch=(), place=pltpu.VMEM):
    return pl.pallas_call(
        body,
        name=name,
        out_shape=outs,
        in_specs=[pl.BlockSpec(memory_space=place)] * len(ins),
        out_specs=[pl.BlockSpec(memory_space=place)] * len(outs),
        scratch_shapes=[*scratch, pltpu.SemaphoreType.DMA((sems,))],
        compiler_params=pltpu.CompilerParams(
            collective_id=collective_id, has_side_effects=True, vmem_limit_bytes=62 << 20
        ),
    )(*ins)


def block_body(
    x_in, pair_in, w_in_in, w_out_in, w_bias_in, w_sides_in, w_outer_in, w_tri_in, w_last_in,
    x_out, pair_out,
    x, pair, w_in, w_out, w_bias, w_sides, w_outer, w_tri, w_last,
    x_new, got, mid, gate, pair_new, xs, bias_out, bias_in, biases, bias, q_all, gates, v_all, scores_all, gated,
    flat, left, right, chunk, lefts, rights, left_s, right_s, tall, stacked, w_wide, normed,
    left_edge, right_edge, spreads, parts, held, mates, sums_0, sums_1, channel_0, channel_1, back_0, back_1,
    outgoing_0, outgoing_1, tiles_0, tiles_1,
    near, far, load, back_sem, sem,
):
    sums, channel, back = (sums_0, sums_1), (channel_0, channel_1), (back_0, back_1)
    outgoing, tiles = (outgoing_0, outgoing_1), (tiles_0, tiles_1)
    r, c = here()
    core = lax.rem(c, 2)
    mate = c + 1 - 2 * core
    mine = c // 2
    parity = lax.rem(r, 2)
    S, B, C = x.shape
    H = w_bias.shape[0]
    D = C // H
    O = w_sides.shape[0] // 2
    Z = pair.shape[2]
    G = B // 4
    P = bias_out.shape[0]
    loads = [
        pltpu.make_async_copy(src, dst, load.at[k])
        for k, (src, dst) in enumerate(
            (
                (pair_in, pair), (w_bias_in, w_bias), (x_in, x), (w_in_in, w_in), (w_out_in, w_out),
                (w_sides_in, w_sides), (w_outer_in, w_outer), (w_tri_in, w_tri),
                (w_last_in, w_last),
            )
        )
    ]
    for cp in loads:
        cp.start()
    for s in range(1, N):
        greet((r, lax.rem(c + s, N)))
    for s in range(1, N):
        greet((lax.rem(r + s, N), c))

    @pl.when(r < P)
    def _():
        for s in range(N):
            k = lax.rem(c + s, N)

            @pl.when((c != r) | (k != c))
            def _():
                greet((c, k))

    for s in range(8):
        k = 2 * lax.rem(mine + s, 8) + core

        @pl.when((k != r) | (r != c))
        def _():
            greet((k, r))

    loads[0].wait()
    loads[1].wait()
    pair_n = standardize(pair[...]).astype(BF).reshape(B * B, Z)
    bias_flat = lax.dot_general(
        w_bias[...], pair_n, (((1,), (1,)), ((), ())), preferred_element_type=F32
    )
    bias_flat = jnp.concatenate([bias_flat, jnp.zeros((H, P * 128 - B * B), F32)], 1).astype(BF)
    for k in range(P):
        bias_out[k] = bias_flat[:, k * 128 : (k + 1) * 128]
    own_p = (r == c) & (r < P)
    greeted(38 + P - jnp.where(r == c, 1, 0) - jnp.where(own_p, 1, 0))
    for s in range(P):
        k = lax.rem(s + c, P)
        own = (k == r) & (r == c)

        @pl.when(jnp.logical_not(own))
        def _():
            push(bias_out.at[k], bias_in.at[c], sem.at[10], sem.at[11], (k, r))

        @pl.when(own)
        def _():
            local(bias_out.at[k], bias_in.at[c], sem.at[11])

    @pl.loop(0, S)
    def _(s):
        for g in AROUND[:-1]:
            push(x_in.at[s], xs.at[s, core, mine], sem.at[12], near.at[s], (r, lax.rem(c + 2 * g, N)))
        local(x_in.at[s], xs.at[s, core, mine], near.at[s])

    @pl.when(r < P)
    def _():
        drain(bias_in, sem.at[11])
        for s in AROUND_16:
            push(bias_in, biases.at[r], sem.at[4], sem.at[5], (lax.rem(r + s, N), c))
        local(bias_in, biases.at[r], sem.at[5])

    def forward(s):
        drain(xs.at[s, core], near.at[s])
        push(xs.at[s, core], xs.at[s, core], sem.at[13], far.at[s], (r, mate))

    for cp in loads[2:]:
        cp.wait()
    own_n = standardize(x[...]).astype(BF).reshape(S * B, C)
    q = jnp.dot(own_n, w_in[:, :C], preferred_element_type=F32) * D ** (-0.5)
    q_all[...] = q.reshape(S, B, C)
    gates[...] = jax.nn.sigmoid(jnp.dot(own_n, w_in[:, 3 * C :], preferred_element_type=F32))
    w_wide[...] = jnp.zeros_like(w_wide)
    tall[pl.ds(0, O * O), :] = w_outer[...].astype(F32)
    for d in range(O):
        part = tall[pl.ds(d, O, stride=O), :].astype(BF)
        for i in range(4):
            w_wide[pl.ds(d * 4 * O + i * O, O), i * Z : (i + 1) * Z] = part
    head = lax.broadcasted_iota(jnp.int32, (B, C), 1) // D
    forward(0)

    @pl.loop(0, S)
    def _(s):
        @pl.when(s < S - 1)
        def _():
            forward(s + 1)

        drain(xs.at[s, 1 - core], far.at[s])
        x_s = standardize(xs[s]).reshape(N * B, C).astype(BF)
        k = jnp.dot(x_s, w_in[:, C : 2 * C], preferred_element_type=F32).astype(BF)
        v_all[s] = jnp.dot(x_s, w_in[:, 2 * C : 3 * C], preferred_element_type=F32).astype(BF)
        q_s = q_all[s]
        q_h = jnp.concatenate([jnp.where(head == h, q_s, 0.0) for h in range(H)], 0).astype(BF)
        scores_all[s] = lax.dot_general(
            q_h, k, (((1,), (1,)), ((), ())), preferred_element_type=F32
        )

    drain(bias_out.at[pl.ds(0, P - 1)], sem.at[10])

    @pl.when(jnp.logical_not(own_p))
    def _():
        drain(bias_out.at[0], sem.at[10])

    @pl.when(r < P)
    def _():
        for s in range(1, N):
            drain(bias_in, sem.at[4])

    drain(biases, sem.at[5])

    def bias_of(k):
        block = 2 * (k % 8) + k // 8
        return jnp.concatenate([biases[p, block].astype(F32) for p in range(P)], 1)

    spread(bias_of, bias, B)
    for first, count in ((0, 3 * S // 4), (3 * S // 4, S // 4)):

        @pl.loop(first, first + count)
        def _(s):
            scores = scores_all[s] + bias[...].reshape(H * B, N * B)
            e = jnp.exp(scores - jnp.max(scores, -1, keepdims=True))
            att = jnp.dot(e.astype(BF), v_all[s], preferred_element_type=F32)
            att = (att / jnp.sum(e, -1, keepdims=True)).reshape(H, B, C)
            total = jnp.where(head == 0, att[0], 0.0)
            for h in range(1, H):
                total = jnp.where(head == h, att[h], total)
            gated[pl.ds(pl.multiple_of(s * B, 8), B), :] = total

        span = slice(first * B, (first + count) * B)
        update = jnp.dot(
            (gated[span] * gates[span]).astype(BF), w_out[...], preferred_element_type=F32
        )
        x_half = (
            x[first : first + count].astype(F32) + update.reshape(count, B, C)
        ).astype(BF)
        x_new[first : first + count] = x_half
        flat[span, : 2 * O] = lax.dot_general(
            standardize(x_half).astype(BF).reshape(count * B, C), w_sides[...],
            (((1,), (1,)), ((), ())), preferred_element_type=F32,
        )
        for k, side in ((0, left), (O, right)):
            lanes = jnp.concatenate(
                [flat[pl.ds(first * B + u, count * G, stride=4), :][:, k : k + O] for u in range(4)], 1
            )
            for s in range(count):
                side[first + s] = lanes[s * G : (s + 1) * G].astype(BF)
        for s in range(first, first + count):
            k = 2 * s + parity
            own = (k == c) & (r == c)

            @pl.when(jnp.logical_not(own))
            def _():
                push(left.at[s], chunk.at[r // 2], sem.at[0], sem.at[1], (c, k))

            @pl.when(own)
            def _():
                local(left.at[s], chunk.at[r // 2], sem.at[1])

        part = right.at[pl.ds(first, count)]
        there = rights.at[parity, pl.ds(first, count), r // 2]
        for s in AROUND_16:
            push(part, there, sem.at[2], sem.at[3], (lax.rem(r + s, N), c))
        local(part, there, sem.at[3])
    x_done = pltpu.make_async_copy(x_new, x_out, load.at[0])
    x_done.start()
    drain(chunk, sem.at[1])
    for s in AROUND[:-1]:
        push(chunk, lefts.at[core, mine], sem.at[6], sem.at[7], (r, lax.rem(c + 2 * s, N)))
    local(chunk, lefts.at[core, mine], sem.at[7])
    for g in range(7):
        drain(xs.at[:, 0, 0], sem.at[12])
    drain(xs.at[:, 0], sem.at[13])
    drain(lefts.at[core], sem.at[7])
    push(lefts.at[core], lefts.at[core], sem.at[8], sem.at[9], (r, mate))
    drain(chunk.at[pl.ds(0, 7)], sem.at[0])

    @pl.when(r != c)
    def _():
        drain(chunk.at[0], sem.at[0])

    for s in range(N - 1):
        drain(right, sem.at[2])
    drain(lefts.at[0, pl.ds(0, 7)], sem.at[6])
    drain(rights, sem.at[3])
    right_s[...] = rights[...].astype(F32).reshape(S * N, G, 4 * O)
    for k in range(G):
        tall[pl.ds(k * 4 * O, 4 * O), :] = right_s[:, k, :].T
    right_t = jnp.concatenate([tall[pl.ds(d, B, stride=O), :] for d in range(O)], 0).astype(BF)
    drain(lefts.at[0], sem.at[8])
    drain(lefts.at[1 - core], sem.at[9])
    left_s[...] = lefts[...].astype(F32).reshape(S * N, G, 4 * O)
    for g in range(B // 8):
        halves = [
            jnp.dot(right_t, left_s[:, k, :].astype(BF), preferred_element_type=F32)
            * (1.0 / (S * N))
            for k in (2 * g, 2 * g + 1)
        ]
        for d in range(O):
            stacked[pl.ds(g * 2 * B, 2 * B), d * 4 * O : (d + 1) * 4 * O] = jnp.concatenate(
                [h[d * B : (d + 1) * B] for h in halves], 0
            ).astype(BF)
    wide = jnp.dot(stacked[...], w_wide[...], preferred_element_type=F32)
    for i in range(B):
        k, u = i // 4, i % 4
        row = (pair[i].astype(F32) + wide[k * B : (k + 1) * B, u * Z : (u + 1) * Z]).astype(BF)
        mid[i] = row
        normed[pl.ds(i * B, B), :] = standardize(row)
    tri_n = normed[...].astype(BF)

    def edge(k):
        w = w_tri[:, 2 * k * Z : 2 * (k + 1) * Z]
        both = lax.dot_general(w, tri_n, (((0,), (1,)), ((), ())), preferred_element_type=F32)
        return (jax.nn.sigmoid(both[Z:]) * both[:Z]).reshape(8, 2, 8, B * B)

    def over_col(k, h):
        ref = (left_edge, right_edge)[k]
        for s in AROUND:
            g = lax.rem(mine + s, 8)
            to = 2 * g + lax.rem(parity + 1 + k, 2)
            if s == 0:

                @pl.when(to != c)
                def _():
                    push(ref.at[h, g], got.at[h, c], back_sem.at[14], back_sem.at[15 + h], (r, to))

                @pl.when(to == c)
                def _():
                    local(ref.at[h, g], got.at[h, c], back_sem.at[15 + h])
            else:
                push(ref.at[h, g], got.at[h, c], back_sem.at[14], back_sem.at[15 + h], (r, to))

    for k, ref in ((0, left_edge), (1, right_edge)):
        values = edge(k)
        for h in range(2):
            ref[h] = values[:, h].astype(BF)
        over_col(k, 0)
    over_col(0, 1)
    over_col(1, 1)
    gate[...] = jax.nn.sigmoid(jnp.dot(tri_n, w_tri[:, 4 * Z :], preferred_element_type=F32))
    kind = lax.rem(r + core, 2)
    R = N * B
    arrived = back_sem.at[1 + 2 * parity + r // 8]
    for h in range(2):
        drain(got.at[h], back_sem.at[15 + h])
        spread(lambda k: got[h, k].astype(F32), spreads, B)
        parts[pl.ds(8 * h, 8)] = spreads[...].astype(BF)
        for s in AROUND:
            q = 8 * h + lax.rem(r + s, 8)
            if s == 0:

                @pl.when(q != r)
                def _():
                    push(parts.at[q], held.at[kind, r // 2], back_sem.at[0], arrived, (q, c))

                @pl.when(q == r)
                def _():
                    local(parts.at[q], held.at[kind, r // 2], arrived)
            else:
                push(parts.at[q], held.at[kind, r // 2], back_sem.at[0], arrived, (q, c))
    for h in range(2):
        some = held.at[1, pl.ds(4 * h, 4)]
        drain(some, back_sem.at[3 - 2 * core + h])
        push(some, mates.at[pl.ds(4 * h, 4)], back_sem.at[5], back_sem.at[6], (r, mate))
    for h in range(2):
        drain(held.at[0, pl.ds(4 * h, 4)], back_sem.at[1 + 2 * core + h])
    columns = held[0].reshape(8 * B, R)
    rows = ((0, B * 3 // 5), (B * 3 // 5, B))

    def products(ref):
        return lax.dot_general(
            ref.reshape(8 * B, R), columns, (((1,), (1,)), ((), ())), preferred_element_type=F32
        )

    def over_row(piece, odd):
        for s in AROUND:
            q = 2 * lax.rem(r // 2 + s, 8) + odd

            @pl.when(q != r)
            def _():
                push(sums[piece].at[q], channel[piece].at[r], back_sem.at[7], back_sem.at[8 + piece], (q, c))

            @pl.when(q == r)
            def _():
                local(sums[piece].at[q], channel[piece].at[r], back_sem.at[8 + piece])

    for ref, odd in ((held.at[1], 1 - core), (mates, core)):
        if ref is mates:
            drain(mates, back_sem.at[6])
        total = products(ref[...])
        for piece, (low, high) in enumerate(rows):
            for s in range(8):
                sums[piece][2 * s + odd] = total[s * B + low : s * B + high].astype(BF)
            if piece == 0:
                over_row(0, odd)
    over_row(1, 1 - core)
    over_row(1, core)
    drain(parts.at[pl.ds(0, N - 1)], back_sem.at[0])
    drain(mates, back_sem.at[5])
    for piece in range(2):
        drain(channel[piece], back_sem.at[8 + piece])
        back[piece][...] = channel[piece][...].astype(F32)
        lines = [back[piece][:, i, :] for i in range(back[piece].shape[1])]
        for g in range(8):
            outgoing[piece][g] = jnp.concatenate([v[:, g * B : (g + 1) * B] for v in lines], 1).astype(BF)
        for s in AROUND[:-1]:
            g = lax.rem(mine + s, 8)
            push(
                outgoing[piece].at[g], tiles[piece].at[mine], back_sem.at[10], back_sem.at[11 + piece],
                (r, 2 * g + core),
            )
        local(outgoing[piece].at[mine], tiles[piece].at[mine], back_sem.at[11 + piece])
    for piece, (low, high) in enumerate(rows):
        drain(tiles[piece], back_sem.at[11 + piece])
        tri_ln = standardize(tiles[piece][...].reshape(Z, (high - low) * B), 0).astype(BF)
        update = lax.dot_general(
            tri_ln, w_last[...], (((0,), (0,)), ((), ())), preferred_element_type=F32
        )
        pair_new[low:high] = (
            mid[low:high].astype(F32)
            + (gate[low * B : high * B, :] * update).reshape(high - low, B, Z)
        ).astype(BF)
    for piece in range(2):
        drain(sums[piece].at[pl.ds(0, N - 1)], back_sem.at[7])
        drain(outgoing[piece].at[pl.ds(0, 7)], back_sem.at[10])
    for h in range(2):
        drain(got.at[h, pl.ds(0, N - 1)], back_sem.at[14])
    done = pltpu.make_async_copy(pair_new, pair_out, back_sem.at[13])
    done.start()
    done.wait()
    x_done.wait()


def spread(block, out, B):
    blocks = [block(k) for k in range(N)]
    for i in range(B):
        out[:, i, :] = jnp.concatenate([b[:, i * B : (i + 1) * B] for b in blocks], 1)


def like(shape, dtype=BF):
    return jax.ShapeDtypeStruct(shape, dtype)


def shards(x, pair, w_in, w_out, w_bias, w_sides, w_outer, w_tri, w_tri_out):
    core = lax.rem(lax.axis_index("col"), 2)
    S, B, C = x.shape
    Z = pair.shape[2]
    H = w_bias.shape[1]
    O = w_sides.shape[1] // 2
    G = B // 4
    SP = S * N
    R = B * N
    P = -(-B * B // 128)
    pieces = (B * 3 // 5, B - B * 3 // 5)

    VM = pltpu.VMEM
    args = [x, pair, w_in, w_out, w_bias.T, w_sides.T, w_outer, w_tri, w_tri_out]
    return comm_call(
        block_body, "block", 1, [like((S, B, C)), like((B, B, Z))], args, 16,
        [*(VM(v.shape, BF) for v in args),
         VM((S, B, C), BF), VM((2, N, 8, B * B), BF), VM((B, B, Z), BF), VM((B * B, Z), F32), VM((B, B, Z), BF),
         VM((S, 2, 8, B, C), BF), VM((P, H, 128), BF), VM((N, H, 128), BF), VM((P, N, H, 128), BF), VM((H, B, R), F32),
         VM((S, B, C), F32), VM((S * B, C), F32), VM((S, R, C), BF), VM((S, H * B, R), F32),
         VM((S * B, C), F32),
         VM((S * B, 128), F32), VM((S, G, 4 * O), BF), VM((S, G, 4 * O), BF), VM((8, G, 4 * O), BF),
         VM((2, S, 8, G, 4 * O), BF), VM((2, S, 8, G, 4 * O), BF), VM((SP, G, 4 * O), F32),
         VM((SP, G, 4 * O), F32), VM((B * O, SP), F32), VM((10 * B, 4 * O * O), BF),
         VM((4 * O * O, 4 * Z), BF), VM((B * B, Z), F32), VM((2, 8, 8, B * B), BF), VM((2, 8, 8, B * B), BF),
         VM((8, B, R), F32), VM((N, B, R), BF), VM((2, 8, B, R), BF), VM((8, B, R), BF),
         *(VM((N, n, 8 * B), t) for t in (BF, BF, F32) for n in pieces),
         *(VM((8, N, n * B), BF) for _ in range(2) for n in pieces),
         pltpu.SemaphoreType.DMA((S,)), pltpu.SemaphoreType.DMA((S,)), pltpu.SemaphoreType.DMA((9,)),
         pltpu.SemaphoreType.DMA((17,))],
        pltpu.HBM,
    )


def solution(mesh):
    tile = PartitionSpec("row", "col", None)
    return jax.shard_map(
        shards,
        mesh=mesh,
        in_specs=(tile, tile) + (PartitionSpec(),) * 7,
        out_specs=(tile, tile),
        check_vma=False,
    )
```
